32 devices in a mesh: sample: 2 (over x), row: 16 (over z, y, core).
Axes of the slice: x: 2, y: 2, z: 4, core: 2. Of those that a mesh axis runs over, the one named last changes fastest.
Arguments:
- sample_index: int32 [2], P('sample'), parts along dimension 0, may hold values from 0 to 32767
- lattice_vector: int32 [1024], replicated, may hold values from 1 to 32767
- mode_table: int32 [2, 1024], replicated, may hold values from -16 to 31, as said below
- connectivity: int32 [3, 32768], replicated, may hold values from 0 to 16639, as said below
- density: bfloat16 [64, 32768], P(None, 'row'), may hold values from -3.5 to 3.5
Outputs:
- potential: float32 [8192, 64], P(('sample', 'row')), parts along dimension 0
The draws below stay inside these ranges and needn't reach their ends.
There are 2 independent parts, one for each index of `sample`. The reference program is written for one: setup_inputs(seed, part) draws one part's arguments, and reference() takes and returns one part's arrays. A program takes and returns all parts, laid end to end along the dimension named above; an argument that names none is the same for every part. Nothing has to cross between parts.
Inputs may be any that keep to these rules, and one draw needn't show every extreme that they name: `mode_table`: the 1024 columns are distinct frequency pairs, the polar one from 0 to 31 and the azimuthal one from -16 to 15. `connectivity`: vertex i * 256 + j lies on latitude cycle i and azimuth j. The columns are the triangles of that grid, two per cell between neighbouring cycles (azimuth wrapping around), each once and oriented with outward normals, in random order.
All inputs are finite; a program needn't handle non-finite values.
Results may differ from the reference program's by a relative error of at most 0.0035.
Values may be sent and summed in bfloat16 or wider, within the bound.
No kernel may reach another device: no remote copies, remote signals or barrier semaphores. Data moves between devices by JAX's collectives and lax.ppermute only.
A program may use at most 256 MiB of HBM per device.

```python
import math
import jax
import jax.numpy as jnp
from jax import lax

COLS = 64
MODES = 1024
NLAT = 32768
NPH = 256
SRC_DEV = 2048
BAND_DEV = 256
PANELS = 32768
BAND = 4096
NT = 65


def quad_layout(key):
    quad_total = (NT - 1) * NPH
    canonical = jnp.arange(2 * quad_total, dtype=jnp.int32)
    shuffled = jax.random.permutation(jax.random.fold_in(key, 11), canonical)
    quad_index = shuffled // 2
    return (quad_index // NPH, quad_index % NPH, shuffled % 2)


def draw_mode_table(key, part):
    chosen = jax.random.permutation(jax.random.fold_in(key, 1), jnp.arange(1024, dtype=jnp.int32))[:MODES]
    polar_freq = chosen // 32
    azim_freq = chosen % 32 - 16
    return jnp.stack([polar_freq, azim_freq]).astype(jnp.int32)


def draw_connectivity(key, part):
    cycle_index, column_index, upper_half = quad_layout(key)
    next_column = (column_index + 1) % NPH
    vertex_aa = cycle_index * NPH + column_index
    vertex_ba = (cycle_index + 1) * NPH + column_index
    vertex_ab = cycle_index * NPH + next_column
    vertex_bb = (cycle_index + 1) * NPH + next_column
    corner_one = jnp.where(upper_half == 0, vertex_aa, vertex_ba)
    corner_two = jnp.where(upper_half == 0, vertex_ba, vertex_bb)
    return jnp.stack([corner_one, corner_two, vertex_ab]).astype(jnp.int32)


def draw_density(key, part):
    cycle_index, column_index, upper_half = quad_layout(key)
    polar_mid = math.pi * (cycle_index.astype(jnp.float32) + 1.5) / (NT + 1)
    azim_mid = 2.0 * math.pi * (column_index.astype(jnp.float32) + 0.5) / NPH
    coef_one = jax.random.uniform(jax.random.fold_in(key, 31), (COLS, 1), jnp.float32, -0.8, 0.8)
    coef_two = jax.random.uniform(jax.random.fold_in(key, 32), (COLS, 1), jnp.float32, -0.8, 0.8)
    phase = jax.random.uniform(jax.random.fold_in(key, 33), (COLS, 1), jnp.float32, -math.pi, math.pi)
    sector_count = 2 ** jax.random.randint(jax.random.fold_in(key, 34), (COLS, 1), 1, 4)
    sector_offset = jax.random.randint(jax.random.fold_in(key, 35), (COLS, 1), 0, NPH)
    sector_index = (column_index[None, :] + sector_offset) % NPH * sector_count // NPH
    sector_sign = (1 - 2 * (sector_index % 2)).astype(jnp.float32)
    smooth = 0.6 + coef_one * jnp.cos(polar_mid)[None, :] + coef_two * jnp.sin(polar_mid)[None, :] * jnp.cos(azim_mid[None, :] - phase)
    level_key = jax.random.fold_in(key, 36)
    rough_key = jax.random.fold_in(key, 37)
    levels = jax.random.uniform(level_key, (COLS, 1), jnp.float32, 0.6, 1.2)
    rough = 0.25 * jnp.clip(jax.random.normal(rough_key, (COLS, PANELS), jnp.float32), -3.0, 3.0)
    return (levels * smooth * sector_sign + rough).astype(jnp.bfloat16)


def with_ends(values, own_key, smallest, high):
    longest = values.shape.index(max(values.shape))
    spots = []
    for shift in (0, 1):
        where = [jax.random.randint(jax.random.fold_in(own_key, axis), (), 0, length) for axis, length in enumerate(values.shape)]
        where[longest] = (where[longest] + shift) % values.shape[longest]
        spots.append(tuple(where))
    return values.at[spots[0]].set(smallest).at[spots[1]].set(high)


def setup_inputs(seed: int = 0, part: int = 0) -> dict:
    key_of = jax.random.split(jax.random.key(seed), 6)
    part_keys = jax.random.split(jax.random.fold_in(key_of[5], part), 6)
    return {
        "sample_index": jax.random.randint(part_keys[0], (1,), 0, NLAT).astype(jnp.int32),
        "lattice_vector": with_ends(jax.random.randint(key_of[1], (MODES,), 1, NLAT), jax.random.fold_in(key_of[1], 1), 1, NLAT - 1).astype(jnp.int32),
        "mode_table": draw_mode_table(jax.random.fold_in(key_of[5], 71), part),
        "connectivity": draw_connectivity(jax.random.fold_in(key_of[5], 71), part),
        "density": draw_density(jax.random.fold_in(key_of[5], 71), part),
    }


def vertex_grid(sample_index, lattice_vector, mode_table, cycle_count):
    lattice_steps = sample_index[0] * lattice_vector % NLAT
    shifts = lattice_steps.astype(jnp.float32) / NLAT - 0.5
    polar_freq = mode_table[0].astype(jnp.float32)
    azim_freq = mode_table[1].astype(jnp.float32)
    mode_coef = 0.8 * shifts / (1.0 + polar_freq + jnp.abs(azim_freq)) ** 2
    polar_angle = math.pi * (jnp.arange(cycle_count, dtype=jnp.float32) + 1.0) / (cycle_count + 1)
    azimuth = 2.0 * math.pi * jnp.arange(NPH, dtype=jnp.float32) / NPH
    polar_phase = polar_angle[:, None] * polar_freq[None, :]
    azim_phase = azim_freq[:, None] * azimuth[None, :]
    cos_part = jnp.dot(jnp.cos(polar_phase) * mode_coef[None, :], jnp.cos(azim_phase), precision=lax.Precision.HIGHEST)
    sin_part = jnp.dot(jnp.sin(polar_phase) * mode_coef[None, :], jnp.sin(azim_phase), precision=lax.Precision.HIGHEST)
    radius = jnp.exp(cos_part - sin_part)
    cycle_sin = jnp.sin(polar_angle)[:, None]
    coord_x = radius * cycle_sin * jnp.cos(azimuth)[None, :]
    coord_y = radius * cycle_sin * jnp.sin(azimuth)[None, :]
    coord_z = radius * jnp.cos(polar_angle)[:, None]
    return jnp.stack([coord_x, coord_y, coord_z]).reshape(3, cycle_count * NPH)

def panel_geometry(vertices, corners):
    corner_one = vertices[:, corners[0]]
    corner_two = vertices[:, corners[1]]
    corner_three = vertices[:, corners[2]]
    centers = (corner_one + corner_two + corner_three) / 3.0
    edge_one = corner_two - corner_one
    edge_two = corner_three - corner_one
    area_vectors = 0.5 * jnp.stack([edge_one[1] * edge_two[2] - edge_one[2] * edge_two[1], edge_one[2] * edge_two[0] - edge_one[0] * edge_two[2], edge_one[0] * edge_two[1] - edge_one[1] * edge_two[0]])
    return (centers, area_vectors)

def kernel_tile(target_centers, target_ids, source_centers, source_areas, source_ids):
    delta_x = target_centers[0][:, None] - source_centers[0][None, :]
    delta_y = target_centers[1][:, None] - source_centers[1][None, :]
    delta_z = target_centers[2][:, None] - source_centers[2][None, :]
    dist_sq = delta_x * delta_x + delta_y * delta_y + delta_z * delta_z
    self_pair = target_ids[:, None] == source_ids[None, :]
    safe_dist = jnp.where(self_pair, 1.0, dist_sq)
    numerator = delta_x * source_areas[0][None, :] + delta_y * source_areas[1][None, :] + delta_z * source_areas[2][None, :]
    kernel_value = numerator / (4.0 * math.pi * safe_dist * jnp.sqrt(safe_dist))
    return jnp.where(self_pair, 0.0, kernel_value).astype(jnp.bfloat16)

def reference(sample_index, lattice_vector, mode_table, connectivity, density):
    vertices = vertex_grid(sample_index, lattice_vector, mode_table, NT)
    centers, area_vectors = panel_geometry(vertices, connectivity)
    source_ids = jnp.arange(PANELS, dtype=jnp.int32)
    band_rows = jnp.arange(BAND, dtype=jnp.int32)
    band_panel = band_rows // BAND_DEV * SRC_DEV + band_rows % BAND_DEV
    block = math.gcd(BAND, 256)

    def one_block(turn):
        first_row = turn * block
        target_ids = lax.dynamic_slice_in_dim(band_panel, first_row, block, 0)
        target_centers = centers[:, target_ids]
        tile = kernel_tile(target_centers, target_ids, centers, area_vectors, source_ids)
        return lax.dot_general(tile, density, (((1,), (1,)), ((), ())), preferred_element_type=jnp.float32)
    sums = lax.map(one_block, jnp.arange(BAND // block, dtype=jnp.int32)).reshape(BAND, COLS)
    local_term = 0.5 * density[:, band_panel].astype(jnp.float32).T
    return local_term + sums
```

```python
import math

import jax
import jax.numpy as jnp
import numpy as np
from jax import lax
from jax.experimental import pallas as pl
from jax.experimental.pallas import tpu as pltpu
from jax.sharding import PartitionSpec as P

NLAT = 32768
NPH = 256
BAND_DEV = 256
FREQS = 32
HALF = 24
FEATS = 128
CHUNK = 1024
SRC_STEP = 1024
TGT_STEP = 1024
VMEM = 56 << 20
F32 = jnp.float32
BF16 = jnp.bfloat16


def split(values):
    first = values.astype(BF16).astype(F32)
    rest = values - first
    second = rest.astype(BF16).astype(F32)
    third = (rest - second).astype(BF16).astype(F32)
    return first, second, third


def split_host(values):
    first = values.astype(jnp.bfloat16).astype(np.float64)
    second = (values - first).astype(jnp.bfloat16).astype(np.float64)
    third = (values - first - second).astype(jnp.bfloat16).astype(np.float64)
    return first, second, third


def trig_tables(cycle_count):
    pitch = -(-cycle_count // 16) * 16
    width = -(-3 * pitch // 128) * 128
    lanes = np.arange(width)
    cycle = lanes % pitch
    piece = lanes // pitch
    inside = (cycle < cycle_count) & (piece < 3)
    polar = np.pi * (cycle + 1.0) / (cycle_count + 1)
    freq = np.arange(FREQS)[:, None]
    polar_table = np.concatenate(
        [np.cos(freq * polar) * inside, -np.sin(freq * polar) * inside], axis=1
    ).astype(np.float32)
    azimuth = 2.0 * np.pi * np.arange(NPH)[:, None] / NPH
    azim_freq = np.arange(FREQS)[None, :] - FREQS // 2
    azim_table = np.concatenate(
        [np.cos(azimuth * azim_freq), np.sin(azimuth * azim_freq)], axis=1
    ).astype(np.float32)
    ring = np.zeros((16, width))
    for row, values in enumerate((np.sin(polar), np.cos(polar))):
        for which, part in enumerate(split_host(values.astype(np.float32).astype(np.float64))):
            ring[row] += part * (inside & (piece == which))
    first_cos = float(np.cos(np.pi / (cycle_count + 1)))
    return pitch, width, polar_table, azim_table, ring.astype(jnp.bfloat16), first_cos


def radius_table(sample, lattice, modes, polar_table, azim_table, width):
    shifts = ((sample * lattice) & (NLAT - 1)).astype(F32) / NLAT - 0.5
    polar_freq = modes[0:1, :]
    azim_freq = modes[1:2, :]
    scale = (1 + polar_freq + jnp.abs(azim_freq)).astype(F32)
    coef = 0.8 * shifts / (scale * scale)
    numbers = lax.broadcasted_iota(jnp.int32, (FREQS, modes.shape[1]), 0)
    at_azim = numbers == azim_freq + FREQS // 2
    at_polar = jnp.where(numbers == polar_freq, 1.0, 0.0).astype(BF16)
    pieces = jnp.concatenate([jnp.where(at_azim, part, 0.0) for part in split(coef)], axis=0)
    grid = lax.dot_general(
        pieces.astype(BF16), at_polar, (((1,), (1,)), ((), ())), preferred_element_type=F32
    )
    grid = grid[:FREQS] + grid[FREQS : 2 * FREQS] + grid[2 * FREQS :]
    both = jnp.dot(grid, polar_table, precision=lax.Precision.HIGHEST, preferred_element_type=F32)
    stacked = jnp.concatenate([both[:, :width], both[:, width:]], axis=0)
    return jnp.exp(
        jnp.dot(azim_table, stacked, precision=lax.Precision.HIGHEST, preferred_element_type=F32)
    )


def azimuth_trig(column):
    quarter = (column + NPH // 8) >> 6
    angle = (column - (quarter << 6)).astype(F32) * (2.0 * math.pi / NPH)
    sq = angle * angle
    sin = angle * (
        1.0 + sq * (-1.0 / 6 + sq * (1.0 / 120 + sq * (-1.0 / 5040 + sq * (1.0 / 362880))))
    )
    cos = 1.0 + sq * (
        -0.5 + sq * (1.0 / 24 + sq * (-1.0 / 720 + sq * (1.0 / 40320 - sq * (1.0 / 3628800))))
    )
    odd = (quarter & 1) == 1
    cos_sign = jnp.where(((quarter + 1) & 2) == 2, -1.0, 1.0)
    sin_sign = jnp.where((quarter & 2) == 2, -1.0, 1.0)
    return jnp.where(odd, sin, cos) * cos_sign, jnp.where(odd, cos, sin) * sin_sign


def lookup(table, cycle, column, pitch, width):
    count = cycle.shape[1]
    hot = jnp.where(
        lax.broadcasted_iota(jnp.int32, (pitch, count), 0) == cycle, 1.0, 0.0
    ).astype(BF16)
    parts = [hot, hot, hot]
    if width > 3 * pitch:
        parts.append(jnp.zeros((width - 3 * pitch, count), BF16))
    found = jnp.dot(table, jnp.concatenate(parts, axis=0), preferred_element_type=F32)
    rows = found[:NPH]
    size = NPH // 2
    while size >= 8:
        rows = jnp.where((column & size) != 0, rows[size:], rows[:size])
        size //= 2
    low = lax.broadcasted_iota(jnp.int32, (8, count), 0) == (column & 7)
    radius = jnp.sum(jnp.where(low, rows, 0.0), axis=0, keepdims=True)
    return radius, found[NPH : NPH + 1], found[NPH + 1 : NPH + 2]


def panels(corners, table, pitch, width):
    column = corners & (NPH - 1)
    cycle = corners >> 8
    cos, sin = azimuth_trig(column)
    points = []
    for c in range(3):
        one = slice(c, c + 1)
        radius, ring_sin, ring_cos = lookup(table, cycle[one], column[one], pitch, width)
        flat = radius * ring_sin
        points.append((flat * cos[one], flat * sin[one], radius * ring_cos))
    centers = [(points[0][d] + points[1][d] + points[2][d]) / 3.0 for d in range(3)]
    one = [points[1][d] - points[0][d] for d in range(3)]
    two = [points[2][d] - points[0][d] for d in range(3)]
    half = 0.5 / (4.0 * math.pi)
    areas = [
        half * (one[(d + 1) % 3] * two[(d + 2) % 3] - one[(d + 2) % 3] * two[(d + 1) % 3])
        for d in range(3)
    ]
    return jnp.concatenate(centers, axis=0), jnp.concatenate(areas, axis=0)


def geometry_kernel(
    row_total, group, sizes, sample_ref, lattice_ref, modes_ref, polar_ref, azim_ref, ring_ref,
    connectivity_ref, dist_ref, flux_ref, target_ref, src_corners, tgt_corners, src_sems, tgt_sems,
):
    pitch, width, first_cos, cycle_count = sizes
    src_total = src_corners.shape[1]
    src_dev = src_total // group
    groups = row_total // group
    row = lax.axis_index("row")
    own_group = row // group
    place = row % group
    copies = []
    for k in range(group):
        first = pl.multiple_of((own_group * group + (place ^ k)) * src_dev, 128)
        copies.append(
            pltpu.make_async_copy(
                connectivity_ref.at[:, pl.ds(first, src_dev)],
                src_corners.at[:, pl.ds(k * src_dev, src_dev)],
                src_sems.at[k],
            )
        )
    for k in range(groups):
        owner = (own_group + k + 1) % groups * group + place
        first = pl.multiple_of(owner * src_dev, 128)
        copies.append(
            pltpu.make_async_copy(
                connectivity_ref.at[:, pl.ds(first, BAND_DEV)],
                tgt_corners.at[:, pl.ds(k * BAND_DEV, BAND_DEV)],
                tgt_sems.at[k],
            )
        )
    for copy in copies:
        copy.start()

    radius = radius_table(
        sample_ref[0], lattice_ref[...], modes_ref[...], polar_ref[...], azim_ref[...], width
    )
    north = jnp.mean(radius[:, 0:1], axis=0, keepdims=True) * first_cos
    south = -jnp.mean(radius[:, cycle_count - 1 : cycle_count], axis=0, keepdims=True) * first_cos
    one, two, three = split(radius)
    lane = lax.broadcasted_iota(jnp.int32, radius.shape, 1)
    radius_pieces = jnp.where(lane < pitch, one, jnp.where(lane < 2 * pitch, two, three))
    table = jnp.concatenate([radius_pieces.astype(BF16), ring_ref[...]], axis=0)
    for copy in copies:
        copy.wait()

    def pieces_of(values):
        return jnp.concatenate(split(values), axis=0)

    def sources(step, carry):
        here = pl.ds(pl.multiple_of(step * CHUNK, CHUNK), CHUNK)
        centers, areas = panels(src_corners[:, here], table, pitch, width)
        upper = centers[2:3] >= 0.0
        offset = centers - jnp.concatenate(
            [jnp.zeros((2, CHUNK), F32), jnp.where(upper, north, south)], axis=0
        )
        square = jnp.sum(offset * offset, axis=0, keepdims=True)
        level = jnp.sum(offset * areas, axis=0, keepdims=True)
        o_one, o_two, o_three = split(-2.0 * offset)
        a_one, a_two, a_three = split(areas)
        ones = jnp.ones((3, CHUNK), F32)
        dist = jnp.concatenate(
            [o_one, o_two, o_three, o_one, o_two, o_one, ones, pieces_of(square)], axis=0
        )
        flux = jnp.concatenate(
            [a_one, a_two, a_three, a_one, a_two, a_one, 0.0 * ones, pieces_of(-level)], axis=0
        )
        for ref, values in ((dist_ref, dist), (flux_ref, flux)):
            both = jnp.concatenate(
                [
                    jnp.where(upper, values, 0.0),
                    jnp.where(upper, 0.0, values),
                    jnp.zeros((FEATS - 2 * HALF, CHUNK), F32),
                ],
                axis=0,
            )
            ref[:, here] = both.astype(BF16)
        return carry

    def targets(step, carry):
        here = pl.ds(pl.multiple_of(step * CHUNK, CHUNK), CHUNK)
        centers, _ = panels(tgt_corners[:, here], table, pitch, width)
        ones = jnp.ones((3, CHUNK), F32)
        rows = []
        for origin in (north, south):
            offset = centers - jnp.concatenate(
                [jnp.zeros((2, CHUNK), F32), jnp.broadcast_to(origin, (1, CHUNK))], axis=0
            )
            square = jnp.sum(offset * offset, axis=0, keepdims=True)
            o_one, o_two, o_three = split(offset)
            rows += [o_one, o_one, o_one, o_two, o_two, o_three, pieces_of(square), ones]
        rows.append(jnp.zeros((FEATS - 2 * HALF, CHUNK), F32))
        target_ref[:, here] = jnp.concatenate(rows, axis=0).astype(BF16)
        return carry

    lax.fori_loop(0, src_total // CHUNK, sources, 0)
    lax.fori_loop(0, tgt_corners.shape[1] // CHUNK, targets, 0)


def geometry(sample_index, lattice_vector, mode_table, connectivity, row_total, group, src_dev):
    cycle_count = src_dev * row_total // (2 * NPH) + 1
    pitch, width, polar_table, azim_table, ring, first_cos = trig_tables(cycle_count)
    groups = row_total // group
    src_total = src_dev * group
    tgt_total = groups * BAND_DEV
    vmem = pl.BlockSpec(memory_space=pltpu.VMEM)

    def kernel(*refs):
        geometry_kernel(row_total, group, (pitch, width, first_cos, cycle_count), *refs)

    return pl.pallas_call(
        kernel,
        out_shape=[
            jax.ShapeDtypeStruct((FEATS, src_total), BF16),
            jax.ShapeDtypeStruct((FEATS, src_total), BF16),
            jax.ShapeDtypeStruct((FEATS, tgt_total), BF16),
        ],
        in_specs=[pl.BlockSpec(memory_space=pltpu.SMEM)] + [vmem] * 5 + [pl.BlockSpec(memory_space=pl.ANY)],
        out_specs=[vmem] * 3,
        scratch_shapes=[
            pltpu.VMEM((3, src_total), jnp.int32),
            pltpu.VMEM((3, tgt_total), jnp.int32),
            pltpu.SemaphoreType.DMA((group,)),
            pltpu.SemaphoreType.DMA((groups,)),
        ],
        compiler_params=pltpu.CompilerParams(vmem_limit_bytes=VMEM),
        name="geometry",
    )(
        sample_index, lattice_vector.reshape(1, -1), mode_table, jnp.asarray(polar_table),
        jnp.asarray(azim_table), jnp.asarray(ring), connectivity,
    )


def pairs_kernel(group, dist_ref, flux_ref, target_ref, *refs):
    density_refs, sums_ref = refs[:group], refs[group]
    src_dev = density_refs[0].shape[1]
    last = pl.program_id(0) == pl.num_programs(0) - 1
    target = target_ref[...]
    diagonal = lax.broadcasted_iota(jnp.int32, (BAND_DEV, BAND_DEV), 0) == lax.broadcasted_iota(
        jnp.int32, (BAND_DEV, BAND_DEV), 1
    )
    sums_ref[...] = jnp.zeros_like(sums_ref)
    for k in range(group):

        def step(turn, carry, k=k):
            inside = pl.multiple_of(turn * SRC_STEP, SRC_STEP)
            here = pl.ds(pl.multiple_of(k * src_dev + turn * SRC_STEP, SRC_STEP), SRC_STEP)
            contract = (((0,), (0,)), ((), ()))
            dist_sq = lax.dot_general(dist_ref[:, here], target, contract, preferred_element_type=F32)
            flux = lax.dot_general(flux_ref[:, here], target, contract, preferred_element_type=F32)
            if k == 0:
                far = jnp.where(last & (turn == 0), 1e30, 0.0)
                apart = jnp.where(diagonal, far, 0.0)
                top = jnp.concatenate(
                    [dist_sq[:BAND_DEV, :-BAND_DEV], dist_sq[:BAND_DEV, -BAND_DEV:] + apart], axis=1
                )
                dist_sq = jnp.concatenate([top, dist_sq[BAND_DEV:]], axis=0)
            inverse = lax.rsqrt(dist_sq)
            tile = (flux * inverse * (inverse * inverse)).astype(BF16)
            sums_ref[...] += jnp.dot(
                density_refs[k][:, pl.ds(inside, SRC_STEP)], tile, preferred_element_type=F32
            )
            return carry

        lax.fori_loop(0, src_dev // SRC_STEP, step, 0)


def pairs(dist, flux, target, densities):
    columns = densities[0].shape[0]
    total = target.shape[1]
    vmem = pl.BlockSpec(memory_space=pltpu.VMEM)

    def kernel(*refs):
        pairs_kernel(len(densities), *refs)

    return pl.pallas_call(
        kernel,
        grid=(total // TGT_STEP,),
        out_shape=jax.ShapeDtypeStruct((columns, total), F32),
        in_specs=[vmem, vmem, pl.BlockSpec((FEATS, TGT_STEP), lambda t: (0, t))]
        + [vmem] * len(densities),
        out_specs=pl.BlockSpec((columns, TGT_STEP), lambda t: (0, t)),
        compiler_params=pltpu.CompilerParams(vmem_limit_bytes=VMEM),
        name="pairs",
    )(dist, flux, target, *densities)


def finish(density, parts):
    def kernel(density_ref, *refs):
        total = 0.5 * density_ref[...].astype(F32)
        for ref in refs[:-1]:
            total = total + ref[...]
        refs[-1][...] = total.T

    columns = density.shape[0]
    block = pl.BlockSpec((columns, BAND_DEV), lambda i: (0, 0))
    return pl.pallas_call(
        kernel,
        grid=(1,),
        out_shape=jax.ShapeDtypeStruct((BAND_DEV, columns), F32),
        in_specs=[block] * (1 + len(parts)),
        out_specs=pl.BlockSpec((BAND_DEV, columns), lambda i: (0, 0)),
        name="finish",
    )(density, *parts)


def per_device(sample_index, lattice_vector, mode_table, connectivity, density):
    src_dev = density.shape[1]
    row_total = lax.axis_size("row")
    group = math.gcd(row_total, 4)
    groups = row_total // group
    densities = [density] + [
        lax.ppermute(density, "row", [(r, r ^ k) for r in range(row_total)])
        for k in range(1, group)
    ]
    dist, flux, target = geometry(
        sample_index, lattice_vector, mode_table, connectivity, row_total, group, src_dev
    )
    sums = pairs(dist, flux, target, densities)
    parts = [sums[:, (groups - 1) * BAND_DEV :]]
    for k in range(1, groups):
        block = sums[:, (k - 1) * BAND_DEV : k * BAND_DEV]
        parts.append(
            lax.ppermute(
                block, "row", [(r, (r + k * group) % row_total) for r in range(row_total)]
            )
        )
    return finish(density, parts)


def solution(mesh):
    placed = (P("sample"), P(), P(), P(), P(None, "row"))
    return jax.shard_map(
        per_device,
        mesh=mesh,
        in_specs=placed,
        out_specs=P(("sample", "row"), None),
        check_vma=False,
    )
```

```python
import math

import jax
import jax.numpy as jnp
import numpy as np
from jax import lax
from jax.experimental import pallas as pl
from jax.experimental.pallas import tpu as pltpu
from jax.sharding import PartitionSpec as P

NLAT = 32768
NPH = 256
BAND_DEV = 256
FREQS = 32
HALF = 24
FEATS = 128
CHUNK = 1024
SRC_STEP = 1024
TGT_STEP = 768
VMEM = 56 << 20
F32 = jnp.float32
BF16 = jnp.bfloat16


def split(values):
    first = values.astype(BF16).astype(F32)
    rest = values - first
    second = rest.astype(BF16).astype(F32)
    third = (rest - second).astype(BF16).astype(F32)
    return first, second, third


def split_host(values):
    first = values.astype(jnp.bfloat16).astype(np.float64)
    second = (values - first).astype(jnp.bfloat16).astype(np.float64)
    third = (values - first - second).astype(jnp.bfloat16).astype(np.float64)
    return first, second, third


def trig_tables(cycle_count):
    pitch = -(-cycle_count // 16) * 16
    width = -(-3 * pitch // 128) * 128
    lanes = np.arange(width)
    cycle = lanes % pitch
    piece = lanes // pitch
    inside = (cycle < cycle_count) & (piece < 3)
    polar = np.pi * (cycle + 1.0) / (cycle_count + 1)
    freq = np.arange(FREQS)[:, None]
    polar_table = np.concatenate(
        [np.cos(freq * polar) * inside, -np.sin(freq * polar) * inside], axis=1
    ).astype(np.float32)
    azimuth = 2.0 * np.pi * np.arange(NPH)[:, None] / NPH
    azim_freq = np.arange(FREQS)[None, :] - FREQS // 2
    azim_table = np.concatenate(
        [np.cos(azimuth * azim_freq), np.sin(azimuth * azim_freq)], axis=1
    ).astype(np.float32)
    ring = np.zeros((16, width))
    for row, values in enumerate((np.sin(polar), np.cos(polar))):
        for which, part in enumerate(split_host(values.astype(np.float32).astype(np.float64))):
            ring[row] += part * (inside & (piece == which))
    first_cos = float(np.cos(np.pi / (cycle_count + 1)))
    return pitch, width, polar_table, azim_table, ring.astype(jnp.bfloat16), first_cos


def radius_table(sample, lattice, modes, polar_table, azim_table, width):
    shifts = ((sample * lattice) & (NLAT - 1)).astype(F32) / NLAT - 0.5
    polar_freq = modes[0:1, :]
    azim_freq = modes[1:2, :]
    scale = (1 + polar_freq + jnp.abs(azim_freq)).astype(F32)
    coef = 0.8 * shifts / (scale * scale)
    numbers = lax.broadcasted_iota(jnp.int32, (FREQS, modes.shape[1]), 0)
    at_azim = numbers == azim_freq + FREQS // 2
    at_polar = jnp.where(numbers == polar_freq, 1.0, 0.0).astype(BF16)
    pieces = jnp.concatenate([jnp.where(at_azim, part, 0.0) for part in split(coef)], axis=0)
    grid = lax.dot_general(
        pieces.astype(BF16), at_polar, (((1,), (1,)), ((), ())), preferred_element_type=F32
    )
    grid = grid[:FREQS] + grid[FREQS : 2 * FREQS] + grid[2 * FREQS :]
    both = jnp.dot(grid, polar_table, precision=lax.Precision.HIGHEST, preferred_element_type=F32)
    stacked = jnp.concatenate([both[:, :width], both[:, width:]], axis=0)
    return jnp.exp(
        jnp.dot(azim_table, stacked, precision=lax.Precision.HIGHEST, preferred_element_type=F32)
    )


def azimuth_trig(column):
    quarter = (column + NPH // 8) >> 6
    angle = (column - (quarter << 6)).astype(F32) * (2.0 * math.pi / NPH)
    sq = angle * angle
    sin = angle * (
        1.0 + sq * (-1.0 / 6 + sq * (1.0 / 120 + sq * (-1.0 / 5040 + sq * (1.0 / 362880))))
    )
    cos = 1.0 + sq * (
        -0.5 + sq * (1.0 / 24 + sq * (-1.0 / 720 + sq * (1.0 / 40320 - sq * (1.0 / 3628800))))
    )
    odd = (quarter & 1) == 1
    cos_sign = jnp.where(((quarter + 1) & 2) == 2, -1.0, 1.0)
    sin_sign = jnp.where((quarter & 2) == 2, -1.0, 1.0)
    return jnp.where(odd, sin, cos) * cos_sign, jnp.where(odd, cos, sin) * sin_sign


def lookup(table, cycle, column, pitch, width):
    count = cycle.shape[1]
    hot = jnp.where(
        lax.broadcasted_iota(jnp.int32, (pitch, count), 0) == cycle, 1.0, 0.0
    ).astype(BF16)
    parts = [hot, hot, hot]
    if width > 3 * pitch:
        parts.append(jnp.zeros((width - 3 * pitch, count), BF16))
    found = jnp.dot(table, jnp.concatenate(parts, axis=0), preferred_element_type=F32)
    rows = found[:NPH]
    size = NPH // 2
    while size >= 8:
        rows = jnp.where((column & size) != 0, rows[size:], rows[:size])
        size //= 2
    low = lax.broadcasted_iota(jnp.int32, (8, count), 0) == (column & 7)
    radius = jnp.sum(jnp.where(low, rows, 0.0), axis=0, keepdims=True)
    return radius, found[NPH : NPH + 1], found[NPH + 1 : NPH + 2]


def panels(corners, table, pitch, width):
    column = corners & (NPH - 1)
    cycle = corners >> 8
    cos, sin = azimuth_trig(column)
    points = []
    for c in range(3):
        one = slice(c, c + 1)
        radius, ring_sin, ring_cos = lookup(table, cycle[one], column[one], pitch, width)
        flat = radius * ring_sin
        points.append((flat * cos[one], flat * sin[one], radius * ring_cos))
    centers = [(points[0][d] + points[1][d] + points[2][d]) / 3.0 for d in range(3)]
    one = [points[1][d] - points[0][d] for d in range(3)]
    two = [points[2][d] - points[0][d] for d in range(3)]
    half = 0.5 / (4.0 * math.pi)
    areas = [
        half * (one[(d + 1) % 3] * two[(d + 2) % 3] - one[(d + 2) % 3] * two[(d + 1) % 3])
        for d in range(3)
    ]
    return jnp.concatenate(centers, axis=0), jnp.concatenate(areas, axis=0)


def geometry_kernel(
    row_total, group, sizes, sample_ref, lattice_ref, modes_ref, polar_ref, azim_ref, ring_ref,
    connectivity_ref, dist_ref, flux_ref, far_ref, own_ref, src_corners, tgt_corners, src_sems, tgt_sems,
):
    pitch, width, first_cos, cycle_count = sizes
    src_total = src_corners.shape[1]
    src_dev = src_total // group
    groups = row_total // group
    row = lax.axis_index("row")
    own_group = row // group
    place = row % group
    copies = []
    for k in range(group):
        first = pl.multiple_of((own_group * group + (place ^ k)) * src_dev, 128)
        copies.append(
            pltpu.make_async_copy(
                connectivity_ref.at[:, pl.ds(first, src_dev)],
                src_corners.at[:, pl.ds(k * src_dev, src_dev)],
                src_sems.at[k],
            )
        )
    for k in range(groups):
        owner = (own_group + k + 1) % groups * group + place
        first = pl.multiple_of(owner * src_dev, 128)
        copies.append(
            pltpu.make_async_copy(
                connectivity_ref.at[:, pl.ds(first, BAND_DEV)],
                tgt_corners.at[:, pl.ds(k * BAND_DEV, BAND_DEV)],
                tgt_sems.at[k],
            )
        )
    for copy in copies:
        copy.start()

    radius = radius_table(
        sample_ref[0], lattice_ref[...], modes_ref[...], polar_ref[...], azim_ref[...], width
    )
    north = jnp.mean(radius[:, 0:1], axis=0, keepdims=True) * first_cos
    south = -jnp.mean(radius[:, cycle_count - 1 : cycle_count], axis=0, keepdims=True) * first_cos
    one, two, three = split(radius)
    lane = lax.broadcasted_iota(jnp.int32, radius.shape, 1)
    radius_pieces = jnp.where(lane < pitch, one, jnp.where(lane < 2 * pitch, two, three))
    table = jnp.concatenate([radius_pieces.astype(BF16), ring_ref[...]], axis=0)
    for copy in copies:
        copy.wait()

    def pieces_of(values):
        return jnp.concatenate(split(values), axis=0)

    def sources(step, carry):
        here = pl.ds(pl.multiple_of(step * CHUNK, CHUNK), CHUNK)
        centers, areas = panels(src_corners[:, here], table, pitch, width)
        upper = centers[2:3] >= 0.0
        offset = centers - jnp.concatenate(
            [jnp.zeros((2, CHUNK), F32), jnp.where(upper, north, south)], axis=0
        )
        square = jnp.sum(offset * offset, axis=0, keepdims=True)
        level = jnp.sum(offset * areas, axis=0, keepdims=True)
        o_one, o_two, o_three = split(-2.0 * offset)
        a_one, a_two, a_three = split(areas)
        ones = jnp.ones((3, CHUNK), F32)
        dist = jnp.concatenate(
            [o_one, o_two, o_three, o_one, o_two, o_one, ones, pieces_of(square)], axis=0
        )
        flux = jnp.concatenate(
            [a_one, a_two, a_three, a_one, a_two, a_one, 0.0 * ones, pieces_of(-level)], axis=0
        )
        for ref, values in ((dist_ref, dist), (flux_ref, flux)):
            both = jnp.concatenate(
                [
                    jnp.where(upper, values, 0.0),
                    jnp.where(upper, 0.0, values),
                    jnp.zeros((FEATS - 2 * HALF, CHUNK), F32),
                ],
                axis=0,
            )
            ref[:, here] = both.astype(BF16)
        return carry

    def targets(corners):
        count = corners.shape[1]
        centers, _ = panels(corners, table, pitch, width)
        ones = jnp.ones((3, count), F32)
        rows = []
        for origin in (north, south):
            offset = centers - jnp.concatenate(
                [jnp.zeros((2, count), F32), jnp.broadcast_to(origin, (1, count))], axis=0
            )
            square = jnp.sum(offset * offset, axis=0, keepdims=True)
            o_one, o_two, o_three = split(offset)
            rows += [o_one, o_one, o_one, o_two, o_two, o_three, pieces_of(square), ones]
        rows.append(jnp.zeros((FEATS - 2 * HALF, count), F32))
        return jnp.concatenate(rows, axis=0).astype(BF16)

    far_total = far_ref.shape[1]
    for first in range(0, far_total, TGT_STEP):
        count = min(TGT_STEP, far_total - first)
        far_ref[:, first : first + count] = targets(tgt_corners[:, first : first + count])
    own_ref[...] = targets(tgt_corners[:, far_total:])
    lax.fori_loop(0, src_total // CHUNK, sources, 0)


def geometry(sample_index, lattice_vector, mode_table, connectivity, row_total, group, src_dev):
    cycle_count = src_dev * row_total // (2 * NPH) + 1
    pitch, width, polar_table, azim_table, ring, first_cos = trig_tables(cycle_count)
    groups = row_total // group
    src_total = src_dev * group
    tgt_total = groups * BAND_DEV
    vmem = pl.BlockSpec(memory_space=pltpu.VMEM)

    def kernel(*refs):
        geometry_kernel(row_total, group, (pitch, width, first_cos, cycle_count), *refs)

    return pl.pallas_call(
        kernel,
        out_shape=[
            jax.ShapeDtypeStruct((FEATS, src_total), BF16),
            jax.ShapeDtypeStruct((FEATS, src_total), BF16),
            jax.ShapeDtypeStruct((FEATS, tgt_total - BAND_DEV), BF16),
            jax.ShapeDtypeStruct((FEATS, BAND_DEV), BF16),
        ],
        in_specs=[pl.BlockSpec(memory_space=pltpu.SMEM)] + [vmem] * 5 + [pl.BlockSpec(memory_space=pl.ANY)],
        out_specs=[vmem] * 4,
        scratch_shapes=[
            pltpu.VMEM((3, src_total), jnp.int32),
            pltpu.VMEM((3, tgt_total), jnp.int32),
            pltpu.SemaphoreType.DMA((group,)),
            pltpu.SemaphoreType.DMA((groups,)),
        ],
        compiler_params=pltpu.CompilerParams(vmem_limit_bytes=VMEM),
        name="geometry",
    )(
        sample_index, lattice_vector.reshape(1, -1), mode_table, jnp.asarray(polar_table),
        jnp.asarray(azim_table), jnp.asarray(ring), connectivity,
    )


def pairs_kernel(group, own, dist_ref, flux_ref, target_ref, *refs):
    density_refs, sums_refs, total_ref = refs[:group], refs[group:-1], refs[-1]
    src_dev = density_refs[0].shape[1]
    tgt_total = target_ref.shape[1]
    width = min(TGT_STEP, tgt_total)
    src_step = min(src_dev, SRC_STEP * TGT_STEP // width // 2 * 2)
    diagonal = lax.broadcasted_iota(jnp.int32, (BAND_DEV, BAND_DEV), 0) == lax.broadcasted_iota(
        jnp.int32, (BAND_DEV, BAND_DEV), 1
    )
    contract = (((0,), (0,)), ((), ()))
    for first in range(0, tgt_total, width):
        target = target_ref[:, first : first + width]
        total_ref[...] = jnp.zeros_like(total_ref)
        for k in range(group):

            def step(turn, carry, k=k, target=target):
                inside = pl.multiple_of(turn * src_step, src_step)
                here = pl.ds(pl.multiple_of(k * src_dev + turn * src_step, src_step), src_step)
                dist_sq = lax.dot_general(
                    dist_ref[:, here], target, contract, preferred_element_type=F32
                )
                flux = lax.dot_general(
                    flux_ref[:, here], target, contract, preferred_element_type=F32
                )
                if own and k == 0:
                    far = jnp.where(turn == 0, 1e30, 0.0)
                    apart = jnp.where(diagonal, far, 0.0)
                    dist_sq = jnp.concatenate(
                        [dist_sq[:BAND_DEV] + apart, dist_sq[BAND_DEV:]], axis=0
                    )
                inverse = lax.rsqrt(dist_sq)
                tile = (flux * inverse * (inverse * inverse)).astype(BF16)
                total_ref[...] += jnp.dot(
                    density_refs[k][:, pl.ds(inside, src_step)], tile, preferred_element_type=F32
                )
                return carry

            lax.fori_loop(0, src_dev // src_step, step, 0)
        for block in range(width // BAND_DEV):
            sums_refs[first // BAND_DEV + block][...] = total_ref[
                :, block * BAND_DEV : (block + 1) * BAND_DEV
            ]


def pairs(dist, flux, target, densities, own):
    columns = densities[0].shape[0]
    total = target.shape[1]
    vmem = pl.BlockSpec(memory_space=pltpu.VMEM)
    blocks = total // BAND_DEV

    def kernel(*refs):
        pairs_kernel(len(densities), own, *refs)

    return pl.pallas_call(
        kernel,
        out_shape=[jax.ShapeDtypeStruct((columns, BAND_DEV), F32)] * blocks,
        in_specs=[vmem] * (3 + len(densities)),
        out_specs=[vmem] * blocks,
        scratch_shapes=[pltpu.VMEM((columns, min(TGT_STEP, total)), F32)],
        compiler_params=pltpu.CompilerParams(vmem_limit_bytes=VMEM),
        cost_estimate=pl.CostEstimate(
            flops=2 * total * dist.shape[1] * 256, bytes_accessed=1 << 20, transcendentals=0
        ),
        name="pairs_own" if own else "pairs_far",
    )(dist, flux, target, *densities)


def per_device(sample_index, lattice_vector, mode_table, connectivity, density):
    src_dev = density.shape[1]
    row_total = lax.axis_size("row")
    group = math.gcd(row_total, 4)
    groups = row_total // group
    densities = [density] + [
        lax.ppermute(density, "row", [(r, r ^ k) for r in range(row_total)])
        for k in range(1, group)
    ]
    dist, flux, target_far, target_own = geometry(
        sample_index, lattice_vector, mode_table, connectivity, row_total, group, src_dev
    )
    sums = pairs(dist, flux, target_far, densities, False)
    parts = [
        lax.ppermute(
            block, "row", [(r, (r + (k + 1) * group) % row_total) for r in range(row_total)]
        )
        for k, block in enumerate(sums)
    ]
    total = 0.5 * density[:, :BAND_DEV].astype(F32)
    total = total + pairs(dist, flux, target_own, densities, True)[0]
    for part in parts:
        total = total + part
    return total.T


def solution(mesh):
    placed = (P("sample"), P(), P(), P(), P(None, "row"))
    return jax.shard_map(
        per_device,
        mesh=mesh,
        in_specs=placed,
        out_specs=P(("sample", "row"), None),
        check_vma=False,
    )
```

```python
import math

import jax
import jax.numpy as jnp
import numpy as np
from jax import lax
from jax.experimental import pallas as pl
from jax.experimental.pallas import tpu as pltpu
from jax.sharding import PartitionSpec as P

NLAT = 32768
NPH = 256
BAND_DEV = 256
FREQS = 32
HALF = 24
FEATS = 2 * HALF
CHUNK = 1024
TGT_STEP = 768
VMEM = 30 << 20
F32 = jnp.float32
BF16 = jnp.bfloat16


def split(values):
    first = values.astype(BF16).astype(F32)
    rest = values - first
    second = rest.astype(BF16).astype(F32)
    third = (rest - second).astype(BF16).astype(F32)
    return first, second, third


def split_host(values):
    first = values.astype(jnp.bfloat16).astype(np.float64)
    second = (values - first).astype(jnp.bfloat16).astype(np.float64)
    third = (values - first - second).astype(jnp.bfloat16).astype(np.float64)
    return first, second, third


def trig_tables(cycle_count):
    pitch = -(-cycle_count // 16) * 16
    width = -(-3 * pitch // 128) * 128
    lanes = np.arange(width)
    cycle = lanes % pitch
    piece = lanes // pitch
    inside = (cycle < cycle_count) & (piece < 3)
    polar = np.pi * (cycle + 1.0) / (cycle_count + 1)
    freq = np.arange(FREQS)[:, None]
    polar_table = np.concatenate(
        [np.cos(freq * polar) * inside, -np.sin(freq * polar) * inside], axis=1
    ).astype(np.float32)
    azimuth = 2.0 * np.pi * np.arange(NPH)[:, None] / NPH
    azim_freq = np.arange(FREQS)[None, :] - FREQS // 2
    azim_table = np.concatenate(
        [np.cos(azimuth * azim_freq), np.sin(azimuth * azim_freq)], axis=1
    ).astype(np.float32)
    ring = np.zeros((16, width))
    for row, values in enumerate((np.sin(polar), np.cos(polar))):
        for which, part in enumerate(split_host(values.astype(np.float32).astype(np.float64))):
            ring[row] += part * (inside & (piece == which))
    first_cos = float(np.cos(np.pi / (cycle_count + 1)))
    return pitch, width, polar_table, azim_table, ring.astype(jnp.bfloat16), first_cos


def radius_table(sample, lattice, modes, polar_table, azim_table, width):
    shifts = ((sample * lattice) & (NLAT - 1)).astype(F32) / NLAT - 0.5
    polar_freq = modes[0:1, :]
    azim_freq = modes[1:2, :]
    scale = (1 + polar_freq + jnp.abs(azim_freq)).astype(F32)
    coef = 0.8 * shifts / (scale * scale)
    numbers = lax.broadcasted_iota(jnp.int32, (FREQS, modes.shape[1]), 0)
    at_azim = numbers == azim_freq + FREQS // 2
    at_polar = jnp.where(numbers == polar_freq, 1.0, 0.0).astype(BF16)
    pieces = jnp.concatenate([jnp.where(at_azim, part, 0.0) for part in split(coef)], axis=0)
    grid = lax.dot_general(
        pieces.astype(BF16), at_polar, (((1,), (1,)), ((), ())), preferred_element_type=F32
    )
    grid = grid[:FREQS] + grid[FREQS : 2 * FREQS] + grid[2 * FREQS :]
    both = jnp.dot(grid, polar_table, precision=lax.Precision.HIGHEST, preferred_element_type=F32)
    stacked = jnp.concatenate([both[:, :width], both[:, width:]], axis=0)
    return jnp.exp(
        jnp.dot(azim_table, stacked, precision=lax.Precision.HIGHEST, preferred_element_type=F32)
    )


def azimuth_trig(column):
    quarter = (column + NPH // 8) >> 6
    angle = (column - (quarter << 6)).astype(F32) * (2.0 * math.pi / NPH)
    sq = angle * angle
    sin = angle * (
        1.0 + sq * (-1.0 / 6 + sq * (1.0 / 120 + sq * (-1.0 / 5040 + sq * (1.0 / 362880))))
    )
    cos = 1.0 + sq * (
        -0.5 + sq * (1.0 / 24 + sq * (-1.0 / 720 + sq * (1.0 / 40320 - sq * (1.0 / 3628800))))
    )
    odd = (quarter & 1) == 1
    cos_sign = jnp.where(((quarter + 1) & 2) == 2, -1.0, 1.0)
    sin_sign = jnp.where((quarter & 2) == 2, -1.0, 1.0)
    return jnp.where(odd, sin, cos) * cos_sign, jnp.where(odd, cos, sin) * sin_sign


def lookup(table, cycle, column, pitch, width):
    count = cycle.shape[1]
    hot = jnp.where(
        lax.broadcasted_iota(jnp.int32, (pitch, count), 0) == cycle, 1.0, 0.0
    ).astype(BF16)
    parts = [hot, hot, hot]
    if width > 3 * pitch:
        parts.append(jnp.zeros((width - 3 * pitch, count), BF16))
    found = jnp.dot(table, jnp.concatenate(parts, axis=0), preferred_element_type=F32)
    rows = found[:NPH]
    size = NPH // 2
    while size >= 8:
        rows = jnp.where((column & size) != 0, rows[size:], rows[:size])
        size //= 2
    low = lax.broadcasted_iota(jnp.int32, (8, count), 0) == (column & 7)
    radius = jnp.sum(jnp.where(low, rows, 0.0), axis=0, keepdims=True)
    return radius, found[NPH : NPH + 1], found[NPH + 1 : NPH + 2]


def panels(corners, table, pitch, width):
    column = corners & (NPH - 1)
    cycle = corners >> 8
    cos, sin = azimuth_trig(column)
    points = []
    for c in range(3):
        one = slice(c, c + 1)
        radius, ring_sin, ring_cos = lookup(table, cycle[one], column[one], pitch, width)
        flat = radius * ring_sin
        points.append((flat * cos[one], flat * sin[one], radius * ring_cos))
    centers = [(points[0][d] + points[1][d] + points[2][d]) / 3.0 for d in range(3)]
    one = [points[1][d] - points[0][d] for d in range(3)]
    two = [points[2][d] - points[0][d] for d in range(3)]
    half = 0.5 / (4.0 * math.pi)
    areas = [
        half * (one[(d + 1) % 3] * two[(d + 2) % 3] - one[(d + 2) % 3] * two[(d + 1) % 3])
        for d in range(3)
    ]
    return jnp.concatenate(centers, axis=0), jnp.concatenate(areas, axis=0)


def pieces_of(values):
    return jnp.concatenate(split(values), axis=0)


def target_features(corners, table, north, south, pitch, width):
    count = corners.shape[1]
    centers, _ = panels(corners, table, pitch, width)
    ones = jnp.ones((3, count), F32)
    rows = []
    for origin in (north, south):
        offset = centers - jnp.concatenate(
            [jnp.zeros((2, count), F32), jnp.broadcast_to(origin, (1, count))], axis=0
        )
        square = jnp.sum(offset * offset, axis=0, keepdims=True)
        one, two, three = split(offset)
        rows += [one, one, one, two, two, three, pieces_of(square), ones]
    return jnp.concatenate(rows, axis=0).astype(BF16)


def source_features(corners, table, north, south, pitch, width):
    count = corners.shape[1]
    centers, areas = panels(corners, table, pitch, width)
    upper = centers[2:3] >= 0.0
    offset = centers - jnp.concatenate(
        [jnp.zeros((2, count), F32), jnp.where(upper, north, south)], axis=0
    )
    square = jnp.sum(offset * offset, axis=0, keepdims=True)
    level = jnp.sum(offset * areas, axis=0, keepdims=True)
    ones = jnp.ones((3, count), F32)
    found = []
    for (one, two, three), flat, last in (
        (split(-2.0 * offset), ones, square),
        (split(areas), 0.0 * ones, -level),
    ):
        values = jnp.concatenate([one, two, three, one, two, one, flat, pieces_of(last)], axis=0)
        both = jnp.concatenate(
            [jnp.where(upper, values, 0.0), jnp.where(upper, 0.0, values)], axis=0
        )
        found.append(both.astype(BF16))
    return found


def pair_sums(dist, flux, target, density, apart=None):
    contract = (((0,), (0,)), ((), ()))
    dist_sq = lax.dot_general(dist, target, contract, preferred_element_type=F32)
    flow = lax.dot_general(flux, target, contract, preferred_element_type=F32)
    if apart is not None:
        dist_sq = jnp.concatenate([dist_sq[:BAND_DEV] + apart, dist_sq[BAND_DEV:]], axis=0)
    inverse = lax.rsqrt(dist_sq)
    tile = (flow * inverse * (inverse * inverse)).astype(BF16)
    return jnp.dot(density, tile, preferred_element_type=F32)


def far_steps(corners_ref, density_ref, target_ref, total_ref, dist_ref, flux_ref, features):
    src_total = corners_ref.shape[1]
    tgt_total = target_ref.shape[1]
    chunk = min(CHUNK, src_total)
    steps = src_total // chunk
    tgt_steps = tgt_total // TGT_STEP if tgt_total % TGT_STEP == 0 else tgt_total // BAND_DEV
    tgt_step = tgt_total // tgt_steps

    def make(turn):
        here = pl.ds(pl.multiple_of(turn * chunk, chunk), chunk)
        dist, flux = features(corners_ref[:, here])
        dist_ref[:, here] = dist
        flux_ref[:, here] = flux
        return dist, flux

    def apply(turn, dist, flux):
        here = pl.ds(pl.multiple_of(turn * chunk, chunk), chunk)
        density = density_ref[:, here]

        def some(step):
            cols = pl.ds(pl.multiple_of(step * tgt_step, 128), tgt_step)
            total_ref[:, cols] += pair_sums(dist, flux, target_ref[:, cols], density)

        if tgt_steps == 1:
            some(0)
        else:
            pl.loop(0, tgt_steps)(some)

    def both(turn, carry):
        apply(turn, *carry)
        return tuple(make(turn + 1))

    apply(steps - 1, *lax.fori_loop(0, steps - 1, both, tuple(make(0))))


def partner(own, k, groups):
    return own ^ (groups - k) if groups & (groups - 1) == 0 else (own + groups - k) % groups


def start_corners(connectivity_ref, corners_ref, sems, firsts, count):
    copies = []
    for k, first in enumerate(firsts):
        copy = pltpu.make_async_copy(
            connectivity_ref.at[:, pl.ds(pl.multiple_of(first, 128), count)],
            corners_ref.at[:, pl.ds(k * count, count)],
            sems.at[k],
        )
        copy.start()
        copies.append(copy)
    return copies


def start_density(density_refs, held_ref, sems):
    copies = []
    for k, ref in enumerate(density_refs):
        count = ref.shape[1]
        copy = pltpu.make_async_copy(ref, held_ref.at[:, pl.ds(k * count, count)], sems.at[k])
        copy.start()
        copies.append(copy)
    return copies


def first_kernel(near, row_total, group, sizes, sample_ref, *refs):
    small_refs, connectivity_ref, density_refs, refs = refs[:5], refs[5], refs[6 : 6 + near], refs[6 + near :]
    (table_ref, origin_ref, far_ref, own_ref, total_ref, dist_ref, flux_ref, rest_ref), refs = refs[:8], refs[8:]
    small, (src_corners, tgt_corners, held_ref, small_sems, src_sems, rest_sems, tgt_sems, density_sems) = (
        refs[:5], refs[5:],
    )
    lattice_ref, modes_ref, polar_ref, azim_ref, ring_ref = small
    pitch, width, first_cos, cycle_count = sizes
    src_dev = src_corners.shape[1] // near
    groups = row_total // group
    row = lax.axis_index("row")
    own_group = row // group
    place = row % group
    first_copies = []
    for k in range(5):
        first_copies.append(pltpu.make_async_copy(small_refs[k], small[k], small_sems.at[k]))
        first_copies[k].start()
    copies = start_corners(
        connectivity_ref, tgt_corners, tgt_sems,
        [(partner(own_group, k + 1, groups) * group + place) * src_dev for k in range(groups)], BAND_DEV,
    )
    copies += start_corners(
        connectivity_ref, src_corners, src_sems,
        [(own_group * group + (place ^ k)) * src_dev for k in range(near)], src_dev,
    )
    copies += start_density(density_refs, held_ref, density_sems)
    rest_copies = start_corners(
        connectivity_ref, rest_ref, rest_sems,
        [(own_group * group + (place ^ k)) * src_dev for k in range(near, group)], src_dev,
    )

    for copy in first_copies:
        copy.wait()
    radius = radius_table(
        sample_ref[0], lattice_ref[...], modes_ref[...], polar_ref[...], azim_ref[...], width
    )
    north = jnp.mean(radius[:, 0:1], axis=0, keepdims=True) * first_cos
    south = -jnp.mean(radius[:, cycle_count - 1 : cycle_count], axis=0, keepdims=True) * first_cos
    origin_ref[0:1] = jnp.broadcast_to(north, (1, 128))
    origin_ref[1:2] = jnp.broadcast_to(south, (1, 128))
    one, two, three = split(radius)
    lane = lax.broadcasted_iota(jnp.int32, radius.shape, 1)
    radius_pieces = jnp.where(lane < pitch, one, jnp.where(lane < 2 * pitch, two, three))
    table_ref[...] = jnp.concatenate([radius_pieces.astype(BF16), ring_ref[...]], axis=0)
    for copy in copies:
        copy.wait()

    far_total = far_ref.shape[1]
    for first in range(0, far_total, TGT_STEP):
        last = min(first + TGT_STEP, far_total)
        far_ref[:, first:last] = target_features(
            tgt_corners[:, first:last], table_ref[...], north, south, pitch, width
        )
    own_ref[...] = target_features(
        tgt_corners[:, far_total:], table_ref[...], north, south, pitch, width
    )
    total_ref[...] = jnp.zeros_like(total_ref)

    def features(corners):
        return source_features(corners, table_ref[...], north, south, pitch, width)

    far_steps(src_corners, held_ref, far_ref, total_ref, dist_ref, flux_ref, features)
    for copy in rest_copies:
        copy.wait()


def second_kernel(near, group, sizes, corners_ref, table_ref, origin_ref, far_ref, part_ref, *refs):
    rest = group - near
    density_refs, refs = refs[:rest], refs[rest:]
    (*sums_refs, dist_ref, flux_ref, held_ref, total_ref, density_sems) = refs
    pitch, width = sizes[:2]
    copies = start_density(density_refs, held_ref, density_sems)
    north = origin_ref[0:1, 0:1]
    south = origin_ref[1:2, 0:1]
    total_ref[...] = part_ref[...]
    for copy in copies:
        copy.wait()

    def features(corners):
        return source_features(corners, table_ref[...], north, south, pitch, width)

    far_steps(corners_ref, held_ref, far_ref, total_ref, dist_ref, flux_ref, features)
    for k, ref in enumerate(sums_refs):
        ref[...] = total_ref[:, k * BAND_DEV : (k + 1) * BAND_DEV]


def own_kernel(group, target_ref, *refs):
    halves, density_refs, (sums_ref, total_ref) = refs[:-2 - group], refs[-2 - group : -2], refs[-2:]
    src_dev = density_refs[0].shape[1]
    target = target_ref[...]
    diagonal = lax.broadcasted_iota(jnp.int32, (BAND_DEV, BAND_DEV), 0) == lax.broadcasted_iota(
        jnp.int32, (BAND_DEV, BAND_DEV), 1
    )
    apart = jnp.where(diagonal, 1e30, 0.0)
    near = halves[0].shape[1] // src_dev
    total = None
    for k in range(group):
        dist_ref, flux_ref = halves[0:2] if k < near else halves[2:4]
        here = slice(k % near * src_dev, (k % near + 1) * src_dev)
        part = pair_sums(
            dist_ref[:, here], flux_ref[:, here], target, density_refs[k][...],
            apart if k == 0 else None,
        )
        total = part if total is None else total + part
    sums_ref[...] = total


def per_device(sample_index, lattice_vector, mode_table, connectivity, density):
    columns, src_dev = density.shape
    row_total = lax.axis_size("row")
    group = 4
    near = 2
    groups = row_total // group
    cycle_count = src_dev * row_total // (2 * NPH) + 1
    pitch, width, polar_table, azim_table, ring, first_cos = trig_tables(cycle_count)
    sizes = (pitch, width, first_cos, cycle_count)
    far_total = (groups - 1) * BAND_DEV
    vmem = pl.BlockSpec(memory_space=pltpu.VMEM)
    hbm = pl.BlockSpec(memory_space=pltpu.HBM)
    anywhere = pl.BlockSpec(memory_space=pl.ANY)
    params = pltpu.CompilerParams(vmem_limit_bytes=VMEM)
    densities = [density] + [
        lax.ppermute(density, "row", [(r, r ^ k) for r in range(row_total)])
        for k in range(1, group)
    ]

    def shape(*dims, dtype=BF16):
        return jax.ShapeDtypeStruct(dims, dtype)

    def in_hbm(array):
        return pltpu.with_memory_space_constraint(array, pltpu.HBM)

    def cost(sources, targets):
        return pl.CostEstimate(
            flops=2 * sources * targets * 256 * 3, bytes_accessed=1 << 20, transcendentals=0
        )

    small = [
        lattice_vector.reshape(1, -1), mode_table, jnp.asarray(polar_table),
        jnp.asarray(azim_table), jnp.asarray(ring),
    ]
    table, origins, far, own, part, dist_near, flux_near, corners = pl.pallas_call(
        lambda *refs: first_kernel(near, row_total, group, sizes, *refs),
        out_shape=[
            shape(NPH + 16, width),
            shape(8, 128, dtype=F32),
            shape(FEATS, far_total),
            shape(FEATS, BAND_DEV),
            shape(columns, far_total, dtype=F32),
            shape(FEATS, near * src_dev),
            shape(FEATS, near * src_dev),
            shape(3, (group - near) * src_dev, dtype=jnp.int32),
        ],
        in_specs=[pl.BlockSpec(memory_space=pltpu.SMEM)] + [hbm] * 7 + [anywhere] * (near - 1),
        out_specs=[vmem] * 8,
        scratch_shapes=[pltpu.VMEM(array.shape, array.dtype) for array in small]
        + [
            pltpu.VMEM((3, near * src_dev), jnp.int32),
            pltpu.VMEM((3, groups * BAND_DEV), jnp.int32),
            pltpu.VMEM((columns, near * src_dev), BF16),
            pltpu.SemaphoreType.DMA((5,)),
            pltpu.SemaphoreType.DMA((near,)),
            pltpu.SemaphoreType.DMA((group - near,)),
            pltpu.SemaphoreType.DMA((groups,)),
            pltpu.SemaphoreType.DMA((near,)),
        ],
        compiler_params=params,
        cost_estimate=cost(near * src_dev, far_total),
        name="first_half",
    )(sample_index, *[in_hbm(array) for array in (*small, connectivity, density)], *densities[1:near])

    rest = group - near
    *sums, dist_rest, flux_rest = pl.pallas_call(
        lambda *refs: second_kernel(near, group, sizes, *refs),
        out_shape=[shape(columns, BAND_DEV, dtype=F32)] * (groups - 1)
        + [shape(FEATS, rest * src_dev)] * 2,
        in_specs=[vmem] * 5 + [anywhere] * rest,
        out_specs=[vmem] * (groups + 1),
        scratch_shapes=[
            pltpu.VMEM((columns, rest * src_dev), BF16),
            pltpu.VMEM((columns, far_total), F32),
            pltpu.SemaphoreType.DMA((rest,)),
        ],
        compiler_params=params,
        cost_estimate=cost(rest * src_dev, far_total),
        name="second_half",
    )(corners, table, origins, far, part, *densities[near:])

    parts = [
        lax.ppermute(
            block,
            "row",
            [
                (r, partner(r // group, k + 1, groups) * group + r % group)
                for r in range(row_total)
            ],
        )
        for k, block in enumerate(sums)
    ]
    own_sums = pl.pallas_call(
        lambda *refs: own_kernel(group, *refs),
        out_shape=shape(columns, BAND_DEV, dtype=F32),
        in_specs=[vmem] * (5 + group),
        out_specs=vmem,
        scratch_shapes=[pltpu.VMEM((columns, BAND_DEV), F32)],
        compiler_params=params,
        cost_estimate=cost(group * src_dev, BAND_DEV),
        name="own_targets",
    )(own, dist_near, flux_near, dist_rest, flux_rest, *densities)
    total = 0.5 * density[:, :BAND_DEV].astype(F32) + own_sums
    for other in parts:
        total = total + other
    return total.T


def solution(mesh):
    placed = (P("sample"), P(), P(), P(), P(None, "row"))
    return jax.shard_map(
        per_device,
        mesh=mesh,
        in_specs=placed,
        out_specs=P(("sample", "row"), None),
        check_vma=False,
    )
```

```python
import math

import jax
import jax.numpy as jnp
import numpy as np
from jax import lax
from jax.experimental import pallas as pl
from jax.experimental.pallas import tpu as pltpu
from jax.sharding import PartitionSpec as P

NLAT = 32768
NPH = 256
BAND_DEV = 256
FREQS = 32
HALF = 24
FEATS = 2 * HALF
BLOCK = 1024
CHUNK = 1024
TGT_STEP = 768
VMEM = 30 << 20
F32 = jnp.float32
BF16 = jnp.bfloat16


def split(values):
    first = values.astype(BF16).astype(F32)
    rest = values - first
    second = rest.astype(BF16).astype(F32)
    third = (rest - second).astype(BF16).astype(F32)
    return [first, second, third]


def trig_tables(cycle_count):
    pitch = -(-cycle_count // 8) * 8
    cycle = np.arange(pitch)[:, None]
    polar = np.pi * (cycle + 1.0) / (cycle_count + 1) * (cycle < cycle_count)
    freq = np.arange(FREQS)[None, :]
    polar_table = np.concatenate([np.cos(freq * polar), -np.sin(freq * polar)], axis=0)
    azimuth = 2.0 * np.pi * np.arange(NPH)[None, :] / NPH
    azim_freq = np.arange(FREQS)[:, None] - FREQS // 2
    azim_table = np.concatenate([np.cos(azimuth * azim_freq), np.sin(azimuth * azim_freq)], axis=0)
    rows = -(-cycle_count // 128)
    ring = np.zeros((2, rows * 128))
    ring[0, :cycle_count] = np.sin(polar[:cycle_count, 0])
    ring[1, :cycle_count] = np.cos(polar[:cycle_count, 0])
    angles = np.concatenate(
        [ring.reshape(-1, 128), np.cos(azimuth).reshape(-1, 128), np.sin(azimuth).reshape(-1, 128)]
    )
    angles = np.concatenate([angles, np.zeros((-len(angles) % 8, 128))])
    first_cos = float(np.cos(np.pi / (cycle_count + 1)))
    tables = [polar_table, azim_table, angles]
    return pitch, first_cos, [table.astype(np.float32) for table in tables]


def radius_table(sample, lattice, modes, polar_table, azim_table, pitch):
    shifts = ((sample * lattice) & (NLAT - 1)).astype(F32) / NLAT - 0.5
    polar_freq = modes[0:1, :]
    azim_freq = modes[1:2, :]
    scale = (1 + polar_freq + jnp.abs(azim_freq)).astype(F32)
    coef = 0.8 * shifts / (scale * scale)
    numbers = lax.broadcasted_iota(jnp.int32, (FREQS, modes.shape[1]), 0)
    at_azim = numbers == azim_freq + FREQS // 2
    at_polar = jnp.where(numbers == polar_freq, 1.0, 0.0).astype(BF16)
    grid = None
    for part in split(coef):
        placed = lax.dot_general(
            at_polar,
            jnp.where(at_azim, part, 0.0).astype(BF16),
            (((1,), (1,)), ((), ())),
            preferred_element_type=F32,
        )
        grid = placed if grid is None else grid + placed
    exact = dict(precision=lax.Precision.HIGHEST, preferred_element_type=F32)
    both = jnp.dot(polar_table, grid, **exact)
    return jnp.exp(
        jnp.dot(both[:pitch], azim_table[:FREQS], **exact)
        + jnp.dot(both[pitch:], azim_table[FREQS:], **exact)
    )


def at_lanes(ref, row, first, lanes):
    values = jnp.broadcast_to(ref[row : row + 1, first : first + 128], lanes.shape)
    return jnp.take_along_axis(values, lanes, axis=1)


def radii(table_ref, column, cycles, cycle_count):
    lanes = column & 127
    right = column >= 128
    levels = (cycle_count - 1).bit_length()
    bits = [[(cycle & (1 << level)) != 0 for level in range(levels)] for cycle in cycles]

    def among(low, level):
        if level == 0:
            left = at_lanes(table_ref, low, 0, lanes)
            return [jnp.where(right, at_lanes(table_ref, low, 128, lanes), left)] * len(cycles)
        half = 1 << (level - 1)
        below = among(low, level - 1)
        if low + half >= cycle_count:
            return below
        above = among(low + half, level - 1)
        return [jnp.where(bit[level - 1], y, x) for bit, x, y in zip(bits, below, above)]

    return among(0, levels)


def angle_of(angles_ref, first, rows, index):
    lanes = index & 127
    found = at_lanes(angles_ref, first, 0, lanes)
    for row in range(1, rows):
        found = jnp.where(index >= 128 * row, at_lanes(angles_ref, first + row, 0, lanes), found)
    return found


def panels(corners, table_ref, angles_ref, cycle_count):
    zero, one, two = [
        jnp.concatenate([corners[c : c + 1, k * 128 : (k + 1) * 128] for k in range(8)], axis=0)
        for c in range(3)
    ]
    last = ((zero ^ one) & (NPH - 1)) == 0
    middle = ((zero ^ two) & (NPH - 1)) == 0
    turned = (
        jnp.where(last, two, jnp.where(middle, one, zero)),
        jnp.where(last, zero, jnp.where(middle, two, one)),
        jnp.where(last, one, jnp.where(middle, zero, two)),
    )
    cycles = [corner >> 8 for corner in turned]
    columns = [turned[0] & (NPH - 1), turned[1] & (NPH - 1)]
    radius = radii(table_ref, columns[0], cycles[:1], cycle_count) + radii(
        table_ref, columns[1], cycles[1:], cycle_count
    )
    rows = -(-cycle_count // 128)
    cos = [angle_of(angles_ref, 2 * rows, 2, column) for column in columns]
    sin = [angle_of(angles_ref, 2 * rows + 2, 2, column) for column in columns]
    points = []
    for c in range(3):
        flat = radius[c] * angle_of(angles_ref, 0, rows, cycles[c])
        side = min(c, 1)
        points.append(
            (flat * cos[side], flat * sin[side], radius[c] * angle_of(angles_ref, rows, rows, cycles[c]))
        )
    centers = [(points[0][d] + points[1][d] + points[2][d]) / 3.0 for d in range(3)]
    one = [points[1][d] - points[0][d] for d in range(3)]
    two = [points[2][d] - points[0][d] for d in range(3)]
    half = 0.5 / (4.0 * math.pi)
    areas = [
        half * (one[(d + 1) % 3] * two[(d + 2) % 3] - one[(d + 2) % 3] * two[(d + 1) % 3])
        for d in range(3)
    ]
    return centers, areas


def as_rows(values, stage_ref):
    for k, value in enumerate(values):
        stage_ref[k * 8 : (k + 1) * 8, :] = value
    blocks = [stage_ref[pl.ds(k, len(values), stride=8), :].astype(BF16) for k in range(8)]
    return jnp.concatenate(blocks, axis=1)


def pieces_of(vector):
    parts = [split(coordinate) for coordinate in vector]
    return [[part[k] for part in parts] for k in range(3)]


def target_features(corners, geometry, stage_ref):
    centers, _ = panels(corners, *geometry[:3])
    ones = jnp.ones((8, 128), F32)
    rows = []
    for origin in geometry[3:]:
        offset = centers[:2] + [centers[2] - origin]
        square = offset[0] * offset[0] + offset[1] * offset[1] + offset[2] * offset[2]
        one, two, three = pieces_of(offset)
        rows += one + one + one + two + two + three + split(square) + [ones] * 3
    return as_rows(rows, stage_ref)


def source_features(corners, geometry, stage_refs):
    centers, areas = panels(corners, *geometry[:3])
    north, south = geometry[3:]
    upper = centers[2] >= 0.0
    offset = centers[:2] + [centers[2] - jnp.where(upper, north, south)]
    square = offset[0] * offset[0] + offset[1] * offset[1] + offset[2] * offset[2]
    level = offset[0] * areas[0] + offset[1] * areas[1] + offset[2] * areas[2]
    zeros = jnp.zeros((8, 128), F32)
    found = []
    for vector, flat, last, stage_ref in (
        ([-2.0 * x for x in offset], zeros + 1.0, square, stage_refs[0]),
        (areas, zeros, -level, stage_refs[1]),
    ):
        one, two, three = pieces_of(vector)
        rows = one + two + three + one + two + one + [flat] * 3 + split(last)
        rows = [jnp.where(upper, x, 0.0) for x in rows] + [jnp.where(upper, 0.0, x) for x in rows]
        found.append(as_rows(rows, stage_ref))
    return found


def pair_sums(dist, flux, target, density, apart=None):
    contract = (((0,), (0,)), ((), ()))
    dist_sq = lax.dot_general(dist, target, contract, preferred_element_type=F32)
    flow = lax.dot_general(flux, target, contract, preferred_element_type=F32)
    if apart is not None:
        dist_sq = jnp.concatenate([dist_sq[:BAND_DEV] + apart, dist_sq[BAND_DEV:]], axis=0)
    inverse = lax.rsqrt(dist_sq)
    tile = (flow * inverse * (inverse * inverse)).astype(BF16)
    return jnp.dot(density, tile, preferred_element_type=F32)


def far_steps(
    corners_ref, density_ref, target_ref, total_ref, dist_ref, flux_ref, geometry, stage_ref
):
    src_total = corners_ref.shape[1]
    tgt_total = target_ref.shape[1]
    chunk = min(CHUNK, src_total)
    steps = src_total // chunk
    tgt_step = max(
        step for step in range(BAND_DEV, TGT_STEP + 1, BAND_DEV) if tgt_total % step == 0
    )
    tgt_steps = tgt_total // tgt_step

    def make(turn):
        here = pl.ds(turn * chunk, chunk)
        corners = corners_ref[:, here]
        blocks = [
            source_features(
                corners[:, k * BLOCK : (k + 1) * BLOCK],
                geometry,
                (stage_ref.at[2 * k], stage_ref.at[2 * k + 1]),
            )
            for k in range(chunk // BLOCK)
        ]
        dist, flux = [jnp.concatenate([block[k] for block in blocks], axis=1) for k in range(2)]
        dist_ref[:, here] = dist
        flux_ref[:, here] = flux
        return dist, flux

    def apply(turn, dist, flux):
        here = pl.ds(turn * chunk, chunk)
        density = density_ref[:, here]

        def some(step):
            cols = pl.ds(pl.multiple_of(step * tgt_step, 128), tgt_step)
            total_ref[:, cols] += pair_sums(dist, flux, target_ref[:, cols], density)

        if tgt_steps == 1:
            some(0)
        else:
            pl.loop(0, tgt_steps)(some)

    kept = make(0)
    for turn in range(steps):
        following = make(turn + 1) if turn + 1 < steps else None
        apply(turn, *kept)
        kept = following


def partner(own, k, groups):
    return own ^ (groups - k) if groups & (groups - 1) == 0 else (own + groups - k) % groups


def start_corners(connectivity_ref, corners_ref, sems, firsts, count):
    copies = []
    for k, first in enumerate(firsts):
        copy = pltpu.make_async_copy(
            connectivity_ref.at[:, pl.ds(pl.multiple_of(first, 128), count)],
            corners_ref.at[:, pl.ds(k * count, count)],
            sems.at[k],
        )
        copy.start()
        copies.append(copy)
    return copies


def start_density(density_refs, held_ref, sems):
    copies = []
    for k, ref in enumerate(density_refs):
        count = ref.shape[1]
        copy = pltpu.make_async_copy(ref, held_ref.at[:, pl.ds(k * count, count)], sems.at[k])
        copy.start()
        copies.append(copy)
    return copies


def first_kernel(near, row_total, group, sizes, sample_ref, *refs):
    small_refs, connectivity_ref, density_refs, refs = refs[:5], refs[5], refs[6 : 6 + near], refs[6 + near :]
    (table_ref, origin_ref, *tgt_refs, dist_ref, flux_ref, rest_ref), refs = refs[:10], refs[10:]
    feature_refs, part_refs = tgt_refs[:3], tgt_refs[3:]
    small, (src_corners, tgt_corners, held_ref, stage_ref, far_ref, total_ref, small_sems, src_sems, rest_sems, tgt_sems, density_sems) = (
        refs[:5], refs[5:],
    )
    lattice_ref, modes_ref, polar_ref, azim_ref, angles_ref = small
    pitch, first_cos, cycle_count = sizes
    src_dev = src_corners.shape[1] // near
    groups = row_total // group
    row = lax.axis_index("row")
    own_group = row // group
    place = row % group
    first_copies = []
    for k in range(5):
        first_copies.append(pltpu.make_async_copy(small_refs[k], small[k], small_sems.at[k]))
        first_copies[k].start()
    copies = start_corners(
        connectivity_ref, tgt_corners, tgt_sems,
        [(partner(own_group, k + 1, groups) * group + place) * src_dev for k in range(groups)], BAND_DEV,
    )
    copies += start_corners(
        connectivity_ref, src_corners, src_sems,
        [(own_group * group + (place ^ k)) * src_dev for k in range(near)], src_dev,
    )
    copies += start_density(density_refs, held_ref, density_sems)
    rest_copies = start_corners(
        connectivity_ref, rest_ref, rest_sems,
        [(own_group * group + (place ^ k)) * src_dev for k in range(near, group)], src_dev,
    )

    for copy in first_copies:
        copy.wait()
    radius = radius_table(
        sample_ref[0], lattice_ref[...], modes_ref[...], polar_ref[...], azim_ref[...], pitch
    )
    north = jnp.mean(radius[0:1], axis=1, keepdims=True) * first_cos
    south = -jnp.mean(radius[cycle_count - 1 : cycle_count], axis=1, keepdims=True) * first_cos
    origin_ref[0:1] = jnp.broadcast_to(north, (1, 128))
    origin_ref[1:2] = jnp.broadcast_to(south, (1, 128))
    table_ref[...] = radius
    for copy in copies:
        copy.wait()

    geometry = (table_ref, angles_ref, cycle_count, north, south)
    found = [
        target_features(tgt_corners[:, first : first + BLOCK], geometry, stage_ref.at[0])
        for first in range(0, tgt_corners.shape[1], BLOCK)
    ]
    found = jnp.concatenate(found, axis=1)
    far_ref[...] = found[:, :-BAND_DEV]
    first = 0
    for ref in feature_refs:
        ref[...] = found[:, first : first + ref.shape[1]]
        first += ref.shape[1]
    total_ref[...] = jnp.zeros_like(total_ref)
    far_steps(
        src_corners, held_ref, far_ref, total_ref, dist_ref, flux_ref, geometry, stage_ref
    )
    first = 0
    for ref in part_refs:
        ref[...] = total_ref[:, first : first + ref.shape[1]]
        first += ref.shape[1]
    for copy in rest_copies:
        copy.wait()


def second_kernel(
    near, group, cycle_count, corners_ref, table_ref, angles_ref, origin_ref, far_ref, part_ref, *refs
):
    rest = group - near
    density_refs, refs = refs[:rest], refs[rest:]
    (*sums_refs, dist_ref, flux_ref, held_ref, total_ref, stage_ref, density_sems) = refs
    copies = start_density(density_refs, held_ref, density_sems)
    geometry = (table_ref, angles_ref, cycle_count, origin_ref[0:1, 0:1], origin_ref[1:2, 0:1])
    total_ref[...] = part_ref[...]
    for copy in copies:
        copy.wait()
    far_steps(corners_ref, held_ref, far_ref, total_ref, dist_ref, flux_ref, geometry, stage_ref)
    for k, ref in enumerate(sums_refs):
        ref[...] = total_ref[:, k * BAND_DEV : (k + 1) * BAND_DEV]


def kept_kernel(own, count, dist_ref, flux_ref, target_ref, *refs):
    density_refs, (*part_refs, sums_ref) = refs[:count], refs[count:]
    src_dev = density_refs[0].shape[1]
    target = target_ref[...]
    apart = None
    if own:
        diagonal = lax.broadcasted_iota(
            jnp.int32, (BAND_DEV, BAND_DEV), 0
        ) == lax.broadcasted_iota(jnp.int32, (BAND_DEV, BAND_DEV), 1)
        apart = jnp.where(diagonal, 1e30, 0.0)
    total = part_refs[0][...] if part_refs else None
    for k in range(count):
        here = slice(k * src_dev, (k + 1) * src_dev)
        sums = pair_sums(
            dist_ref[:, here], flux_ref[:, here], target, density_refs[k][...], None if k else apart
        )
        total = sums if total is None else total + sums
    sums_ref[...] = total


def per_device(sample_index, lattice_vector, mode_table, connectivity, density):
    columns, src_dev = density.shape
    row_total = lax.axis_size("row")
    group = 4
    near = 2
    groups = row_total // group
    cycle_count = src_dev * row_total // (2 * NPH) + 1
    pitch, first_cos, tables = trig_tables(cycle_count)
    sizes = (pitch, first_cos, cycle_count)
    far_total = (groups - 1) * BAND_DEV
    vmem = pl.BlockSpec(memory_space=pltpu.VMEM)
    hbm = pl.BlockSpec(memory_space=pltpu.HBM)
    anywhere = pl.BlockSpec(memory_space=pl.ANY)
    params = pltpu.CompilerParams(vmem_limit_bytes=VMEM)
    def moved(array, target_of):
        return lax.ppermute(array, "row", [(r, target_of(r)) for r in range(row_total)])

    densities = [density, moved(density, lambda r: r ^ 1), moved(density, lambda r: r ^ 2)]

    def shape(*dims, dtype=BF16):
        return jax.ShapeDtypeStruct(dims, dtype)

    def in_hbm(array):
        return pltpu.with_memory_space_constraint(array, pltpu.HBM)

    def cost(sources, targets):
        return pl.CostEstimate(
            flops=2 * sources * targets * 256 * 3, bytes_accessed=1 << 20, transcendentals=0
        )

    small = [lattice_vector.reshape(1, -1), mode_table, *map(jnp.asarray, tables)]
    stage = pltpu.VMEM((2 * min(CHUNK, src_dev) // BLOCK, 8 * FEATS, 128), F32)
    early = far_total - BAND_DEV
    table, origins, tgt_early, tgt_late, tgt_own, part_early, part_late, *near_features, corners = (
        pl.pallas_call(
            lambda *refs: first_kernel(near, row_total, group, sizes, *refs),
            out_shape=[
                shape(pitch, NPH, dtype=F32),
                shape(8, 128, dtype=F32),
                shape(FEATS, early),
                shape(FEATS, BAND_DEV),
                shape(FEATS, BAND_DEV),
                shape(columns, early, dtype=F32),
                shape(columns, BAND_DEV, dtype=F32),
                shape(FEATS, near * src_dev),
                shape(FEATS, near * src_dev),
                shape(3, (group - near) * src_dev, dtype=jnp.int32),
            ],
            in_specs=[pl.BlockSpec(memory_space=pltpu.SMEM)] + [hbm] * 7 + [anywhere] * (near - 1),
            out_specs=[vmem] * 10,
            scratch_shapes=[pltpu.VMEM(array.shape, array.dtype) for array in small]
            + [
                pltpu.VMEM((3, near * src_dev), jnp.int32),
                pltpu.VMEM((3, groups * BAND_DEV), jnp.int32),
                pltpu.VMEM((columns, near * src_dev), BF16),
                stage,
                pltpu.VMEM((FEATS, far_total), BF16),
                pltpu.VMEM((columns, far_total), F32),
                pltpu.SemaphoreType.DMA((5,)),
                pltpu.SemaphoreType.DMA((near,)),
                pltpu.SemaphoreType.DMA((group - near,)),
                pltpu.SemaphoreType.DMA((groups,)),
                pltpu.SemaphoreType.DMA((near,)),
            ],
            compiler_params=params,
            cost_estimate=cost(near * src_dev, far_total),
            name="near_sources",
        )(
            sample_index,
            *[in_hbm(array) for array in (*small, connectivity, density)],
            *densities[1:near],
        )
    )

    relay, origins = lax.optimization_barrier((densities[2], origins))
    densities.append(moved(relay, lambda r: r ^ 1))
    rest = group - near
    *sums, dist_rest, flux_rest = pl.pallas_call(
        lambda *refs: second_kernel(near, group, cycle_count, *refs),
        out_shape=[shape(columns, BAND_DEV, dtype=F32)] * (groups - 2)
        + [shape(FEATS, rest * src_dev)] * 2,
        in_specs=[vmem] * 6 + [anywhere] * rest,
        out_specs=[vmem] * groups,
        scratch_shapes=[
            pltpu.VMEM((columns, rest * src_dev), BF16),
            pltpu.VMEM((columns, early), F32),
            stage,
            pltpu.SemaphoreType.DMA((rest,)),
        ],
        compiler_params=params,
        cost_estimate=cost(rest * src_dev, early),
        name="other_sources",
    )(corners, table, small[4], origins, tgt_early, part_early, *densities[near:])

    def kept(features, target, blocks, own, part):
        return pl.pallas_call(
            lambda *refs: kept_kernel(own, len(blocks), *refs),
            out_shape=shape(columns, BAND_DEV, dtype=F32),
            in_specs=[vmem] * (3 + len(blocks) + len(part)),
            out_specs=vmem,
            compiler_params=params,
            cost_estimate=cost(len(blocks) * src_dev, BAND_DEV),
            name="own_targets" if own else "late_targets",
        )(*features, target, *blocks, *part)

    rest_features = (dist_rest, flux_rest)
    own_sums = kept(near_features, tgt_own, densities[:near], True, [])
    sums.append(kept(rest_features, tgt_late, densities[near:], False, [part_late]))
    own_sums = kept(rest_features, tgt_own, densities[near:], False, [own_sums])
    total = 0.5 * density[:, :BAND_DEV].astype(F32) + own_sums
    for k, block in enumerate(sums):
        total = total + moved(
            block, lambda r, k=k: partner(r // group, k + 1, groups) * group + r % group
        )
    return total.T


def solution(mesh):
    placed = (P("sample"), P(), P(), P(), P(None, "row"))
    return jax.shard_map(
        per_device,
        mesh=mesh,
        in_specs=placed,
        out_specs=P(("sample", "row"), None),
        check_vma=False,
    )
```

```python
import math

import jax
import jax.numpy as jnp
import numpy as np
from jax import lax
from jax.experimental import pallas as pl
from jax.experimental.pallas import tpu as pltpu
from jax.sharding import PartitionSpec as P

NLAT = 32768
NPH = 256
BAND_DEV = 256
FREQS = 32
FEATS = 64
BLOCK = 1024
CHUNK = 1024
TGT_STEP = 768
VMEM = 30 << 20
F32 = jnp.float32
BF16 = jnp.bfloat16


def split(values):
    first = values.astype(BF16).astype(F32)
    rest = values - first
    second = rest.astype(BF16).astype(F32)
    third = (rest - second).astype(BF16).astype(F32)
    return [first, second, third]


def trig_tables(cycle_count):
    pitch = -(-cycle_count // 8) * 8
    cycle = np.arange(pitch)[:, None]
    polar = np.pi * (cycle + 1.0) / (cycle_count + 1) * (cycle < cycle_count)
    freq = np.arange(FREQS)[None, :]
    polar_table = np.concatenate([np.cos(freq * polar), -np.sin(freq * polar)], axis=0)
    azimuth = 2.0 * np.pi * np.arange(NPH)[None, :] / NPH
    azim_freq = np.arange(FREQS)[:, None] - FREQS // 2
    azim_table = np.concatenate([np.cos(azimuth * azim_freq), np.sin(azimuth * azim_freq)], axis=0)
    rows = -(-cycle_count // 128)
    ring = np.zeros((2, rows * 128))
    ring[0, :cycle_count] = np.sin(polar[:cycle_count, 0])
    ring[1, :cycle_count] = np.cos(polar[:cycle_count, 0])
    angles = np.concatenate(
        [ring.reshape(-1, 128), np.cos(azimuth).reshape(-1, 128), np.sin(azimuth).reshape(-1, 128)]
    )
    angles = np.concatenate([angles, np.zeros((-len(angles) % 8, 128))])
    first_cos = float(np.cos(np.pi / (cycle_count + 1)))
    tables = [polar_table, azim_table, angles]
    return pitch, first_cos, [table.astype(np.float32) for table in tables]


def radius_table(sample, lattice, modes, polar_table, azim_table, pitch):
    shifts = ((sample * lattice) & (NLAT - 1)).astype(F32) / NLAT - 0.5
    polar_freq = modes[0:1, :]
    azim_freq = modes[1:2, :]
    scale = (1 + polar_freq + jnp.abs(azim_freq)).astype(F32)
    coef = 0.8 * shifts / (scale * scale)
    numbers = lax.broadcasted_iota(jnp.int32, (FREQS, modes.shape[1]), 0)
    at_azim = numbers == azim_freq + FREQS // 2
    at_polar = jnp.where(numbers == polar_freq, 1.0, 0.0).astype(BF16)
    grid = None
    for part in split(coef):
        placed = lax.dot_general(
            at_polar,
            jnp.where(at_azim, part, 0.0).astype(BF16),
            (((1,), (1,)), ((), ())),
            preferred_element_type=F32,
        )
        grid = placed if grid is None else grid + placed
    exact = dict(precision=lax.Precision.HIGHEST, preferred_element_type=F32)
    both = jnp.dot(polar_table, grid, **exact)
    return jnp.exp(
        jnp.dot(both[:pitch], azim_table[:FREQS], **exact)
        + jnp.dot(both[pitch:], azim_table[FREQS:], **exact)
    )


def heights(first, last, first_cos):
    found, limits = [], []
    for ring, sign in ((first, first_cos), (last, -first_cos)):
        low = jnp.min(ring, axis=1, keepdims=True) * sign
        high = jnp.max(ring, axis=1, keepdims=True) * sign
        found += [0.25 * low + 0.75 * high, 0.75 * low + 0.25 * high]
        limits.append(0.5 * (low + high))
    return found + limits


def at_lanes(ref, row, first, lanes):
    values = jnp.broadcast_to(ref[row : row + 1, first : first + 128], lanes.shape)
    return jnp.take_along_axis(values, lanes, axis=1)


def radii(table_ref, column, cycles, cycle_count):
    lanes = column & 127
    right = column >= 128
    levels = (cycle_count - 1).bit_length()
    bits = [[(cycle & (1 << level)) != 0 for level in range(levels)] for cycle in cycles]

    def among(low, level):
        if level == 0:
            left = at_lanes(table_ref, low, 0, lanes)
            return [jnp.where(right, at_lanes(table_ref, low, 128, lanes), left)] * len(cycles)
        half = 1 << (level - 1)
        below = among(low, level - 1)
        if low + half >= cycle_count:
            return below
        above = among(low + half, level - 1)
        return [jnp.where(bit[level - 1], y, x) for bit, x, y in zip(bits, below, above)]

    return among(0, levels)


def angle_of(angles_ref, first, rows, index):
    lanes = index & 127
    found = at_lanes(angles_ref, first, 0, lanes)
    for row in range(1, rows):
        found = jnp.where(index >= 128 * row, at_lanes(angles_ref, first + row, 0, lanes), found)
    return found


def panels(corners, table_ref, angles_ref, cycle_count):
    zero, one, two = [
        jnp.concatenate([corners[c : c + 1, k * 128 : (k + 1) * 128] for k in range(8)], axis=0)
        for c in range(3)
    ]
    last = ((zero ^ one) & (NPH - 1)) == 0
    middle = ((zero ^ two) & (NPH - 1)) == 0
    turned = (
        jnp.where(last, two, jnp.where(middle, one, zero)),
        jnp.where(last, zero, jnp.where(middle, two, one)),
        jnp.where(last, one, jnp.where(middle, zero, two)),
    )
    cycles = [corner >> 8 for corner in turned]
    columns = [turned[0] & (NPH - 1), turned[1] & (NPH - 1)]
    radius = radii(table_ref, columns[0], cycles[:1], cycle_count) + radii(
        table_ref, columns[1], cycles[1:], cycle_count
    )
    rows = -(-cycle_count // 128)
    cos = [angle_of(angles_ref, 2 * rows, 2, column) for column in columns]
    sin = [angle_of(angles_ref, 2 * rows + 2, 2, column) for column in columns]
    points = []
    for c in range(3):
        flat = radius[c] * angle_of(angles_ref, 0, rows, cycles[c])
        side = min(c, 1)
        points.append(
            (flat * cos[side], flat * sin[side], radius[c] * angle_of(angles_ref, rows, rows, cycles[c]))
        )
    centers = [(points[0][d] + points[1][d] + points[2][d]) / 3.0 for d in range(3)]
    one = [points[1][d] - points[0][d] for d in range(3)]
    two = [points[2][d] - points[0][d] for d in range(3)]
    half = 0.5 / (4.0 * math.pi)
    areas = [
        half * (one[(d + 1) % 3] * two[(d + 2) % 3] - one[(d + 2) % 3] * two[(d + 1) % 3])
        for d in range(3)
    ]
    return centers, areas


def as_rows(values, stage_ref):
    for k, value in enumerate(values):
        stage_ref[k * 8 : (k + 1) * 8, :] = value
    blocks = [stage_ref[pl.ds(k, len(values), stride=8), :].astype(BF16) for k in range(8)]
    return jnp.concatenate(blocks, axis=1)


def left_pieces(value):
    one, two, three = split(value)
    return [one, one, one, two, two, three]


def right_pieces(value):
    one, two, three = split(value)
    return [one, two, three, one, two, one]


def padded(rows):
    return rows + [jnp.zeros((8, 128), F32)] * (FEATS - len(rows))


def target_features(corners, geometry, stage_ref):
    (x, y, z), _ = panels(corners, *geometry[:3])
    ones = [jnp.ones((8, 128), F32)] * 3
    rows = left_pieces(x) + left_pieces(y) + split(x * x + y * y) + ones
    for height in geometry[3][:4]:
        rise = z - height
        rows += left_pieces(rise) + split(rise * rise)
    return as_rows(padded(rows), stage_ref)


def source_features(corners, geometry, stage_refs):
    (x, y, z), areas = panels(corners, *geometry[:3])
    *levels, north, south = geometry[3]
    upper = z >= 0.0
    places = [z >= north, upper & (z < north), z <= south, ~upper & (z > south)]
    height = jnp.where(
        upper, jnp.where(places[0], levels[0], levels[1]), jnp.where(places[2], levels[2], levels[3])
    )
    rise = z - height
    zeros = jnp.zeros((8, 128), F32)
    square = x * x + y * y + rise * rise
    level = x * areas[0] + y * areas[1] + rise * areas[2]
    found = []
    for (a, b, c), flat, last, stage_ref in (
        ((-2.0 * x, -2.0 * y, -2.0 * rise), zeros + 1.0, square, stage_refs[0]),
        (areas, zeros, -level, stage_refs[1]),
    ):
        rows = right_pieces(a) + right_pieces(b) + [flat] * 3 + split(last)
        along = right_pieces(c) + [flat] * 3
        for place in places:
            rows += [jnp.where(place, row, 0.0) for row in along]
        found.append(as_rows(padded(rows), stage_ref))
    return found


def pair_sums(dist, flux, target, density, apart=None):
    contract = (((0,), (0,)), ((), ()))
    dist_sq = lax.dot_general(dist, target, contract, preferred_element_type=F32)
    flow = lax.dot_general(flux, target, contract, preferred_element_type=F32)
    if apart is not None:
        dist_sq = jnp.concatenate([dist_sq[:BAND_DEV] + apart, dist_sq[BAND_DEV:]], axis=0)
    tile = (flow * lax.rsqrt(dist_sq * dist_sq * dist_sq)).astype(BF16)
    return jnp.dot(density, tile, preferred_element_type=F32)


def far_steps(
    corners_ref, density_ref, target_ref, total_ref, dist_ref, flux_ref, geometry, stage_ref
):
    src_total = corners_ref.shape[1]
    tgt_total = target_ref.shape[1]
    chunk = min(CHUNK, src_total)
    steps = src_total // chunk
    tgt_step = max(
        step for step in range(BAND_DEV, TGT_STEP + 1, BAND_DEV) if tgt_total % step == 0
    )
    tgt_steps = tgt_total // tgt_step

    def make(turn):
        here = pl.ds(turn * chunk, chunk)
        corners = corners_ref[:, here]
        blocks = [
            source_features(
                corners[:, k * BLOCK : (k + 1) * BLOCK],
                geometry,
                (stage_ref.at[2 * k], stage_ref.at[2 * k + 1]),
            )
            for k in range(chunk // BLOCK)
        ]
        dist, flux = [jnp.concatenate([block[k] for block in blocks], axis=1) for k in range(2)]
        dist_ref[:, here] = dist
        flux_ref[:, here] = flux
        return dist, flux

    def apply(turn, dist, flux):
        here = pl.ds(turn * chunk, chunk)
        density = density_ref[:, here]

        def some(step):
            cols = pl.ds(pl.multiple_of(step * tgt_step, 128), tgt_step)
            total_ref[:, cols] += pair_sums(dist, flux, target_ref[:, cols], density)

        if tgt_steps == 1:
            some(0)
        else:
            pl.loop(0, tgt_steps)(some)

    kept = make(0)
    for turn in range(steps):
        following = make(turn + 1) if turn + 1 < steps else None
        apply(turn, *kept)
        kept = following


def partner(own, k, groups):
    return own ^ (groups - k) if groups & (groups - 1) == 0 else (own + groups - k) % groups


def start_corners(connectivity_ref, corners_ref, sems, firsts, count):
    copies = []
    for k, first in enumerate(firsts):
        copy = pltpu.make_async_copy(
            connectivity_ref.at[:, pl.ds(pl.multiple_of(first, 128), count)],
            corners_ref.at[:, pl.ds(k * count, count)],
            sems.at[k],
        )
        copy.start()
        copies.append(copy)
    return copies


def start_density(density_refs, held_ref, sems):
    copies = []
    for k, ref in enumerate(density_refs):
        count = ref.shape[1]
        copy = pltpu.make_async_copy(ref, held_ref.at[:, pl.ds(k * count, count)], sems.at[k])
        copy.start()
        copies.append(copy)
    return copies


def first_kernel(near, row_total, group, sizes, sample_ref, *refs):
    small_refs, connectivity_ref, density_refs, refs = refs[:5], refs[5], refs[6 : 6 + near], refs[6 + near :]
    (table_ref, origin_ref, *tgt_refs, dist_ref, flux_ref, rest_ref), refs = refs[:10], refs[10:]
    feature_refs, part_refs = tgt_refs[:3], tgt_refs[3:]
    small, (src_corners, tgt_corners, held_ref, stage_ref, far_ref, total_ref, small_sems, src_sems, rest_sems, tgt_sems, density_sems) = (
        refs[:5], refs[5:],
    )
    lattice_ref, modes_ref, polar_ref, azim_ref, angles_ref = small
    pitch, first_cos, cycle_count = sizes
    src_dev = src_corners.shape[1] // near
    groups = row_total // group
    row = lax.axis_index("row")
    own_group = row // group
    place = row % group
    first_copies = []
    for k in range(5):
        first_copies.append(pltpu.make_async_copy(small_refs[k], small[k], small_sems.at[k]))
        first_copies[k].start()
    copies = start_corners(
        connectivity_ref, tgt_corners, tgt_sems,
        [(partner(own_group, k + 1, groups) * group + place) * src_dev for k in range(groups)], BAND_DEV,
    )
    copies += start_corners(
        connectivity_ref, src_corners, src_sems,
        [(own_group * group + (place ^ k)) * src_dev for k in range(near)], src_dev,
    )
    copies += start_density(density_refs, held_ref, density_sems)
    rest_copies = start_corners(
        connectivity_ref, rest_ref, rest_sems,
        [(own_group * group + (place ^ k)) * src_dev for k in range(near, group)], src_dev,
    )

    for copy in first_copies:
        copy.wait()
    radius = radius_table(
        sample_ref[0], lattice_ref[...], modes_ref[...], polar_ref[...], azim_ref[...], pitch
    )
    rows = angles_ref.shape[0]
    origin_ref[0:rows] = angles_ref[...]
    levels = heights(radius[0:1], radius[cycle_count - 1 : cycle_count], first_cos)
    for k, level in enumerate(levels):
        origin_ref[rows + k : rows + k + 1] = jnp.broadcast_to(level, (1, 128))
    table_ref[...] = radius
    for copy in copies:
        copy.wait()

    geometry = (table_ref, angles_ref, cycle_count, levels)
    found = [
        target_features(tgt_corners[:, first : first + BLOCK], geometry, stage_ref.at[0])
        for first in range(0, tgt_corners.shape[1], BLOCK)
    ]
    found = jnp.concatenate(found, axis=1)
    far_ref[...] = found[:, :-BAND_DEV]
    first = 0
    for ref in feature_refs:
        ref[...] = found[:, first : first + ref.shape[1]]
        first += ref.shape[1]
    total_ref[...] = jnp.zeros_like(total_ref)
    far_steps(
        src_corners, held_ref, far_ref, total_ref, dist_ref, flux_ref, geometry, stage_ref
    )
    first = 0
    for ref in part_refs:
        ref[...] = total_ref[:, first : first + ref.shape[1]]
        first += ref.shape[1]
    for copy in rest_copies:
        copy.wait()


def second_kernel(
    near, group, cycle_count, corners_ref, table_ref, origin_ref, far_ref, part_ref, *refs
):
    rest = group - near
    density_refs, refs = refs[:rest], refs[rest:]
    (*sums_refs, dist_ref, flux_ref, held_ref, total_ref, stage_ref, density_sems) = refs
    copies = start_density(density_refs, held_ref, density_sems)
    rows = origin_ref.shape[0] - 8
    levels = [origin_ref[rows + k : rows + k + 1, 0:1] for k in range(6)]
    geometry = (table_ref, origin_ref, cycle_count, levels)
    total_ref[...] = part_ref[...]
    for copy in copies:
        copy.wait()
    far_steps(corners_ref, held_ref, far_ref, total_ref, dist_ref, flux_ref, geometry, stage_ref)
    for k, ref in enumerate(sums_refs):
        ref[...] = total_ref[:, k * BAND_DEV : (k + 1) * BAND_DEV].astype(BF16)


def kept_kernel(own, count, dist_ref, flux_ref, target_ref, *refs):
    density_refs, (*part_refs, sums_ref) = refs[:count], refs[count:]
    src_dev = density_refs[0].shape[1]
    target = target_ref[...]
    apart = None
    if own:
        diagonal = lax.broadcasted_iota(
            jnp.int32, (BAND_DEV, BAND_DEV), 0
        ) == lax.broadcasted_iota(jnp.int32, (BAND_DEV, BAND_DEV), 1)
        apart = jnp.where(diagonal, 1e30, 0.0)
    total = part_refs[0][...] if part_refs else None
    for k in range(count):
        here = slice(k * src_dev, (k + 1) * src_dev)
        sums = pair_sums(
            dist_ref[:, here], flux_ref[:, here], target, density_refs[k][...], None if k else apart
        )
        total = sums if total is None else total + sums
    sums_ref[...] = total.astype(sums_ref.dtype)


def per_device(sample_index, lattice_vector, mode_table, connectivity, density):
    columns, src_dev = density.shape
    row_total = lax.axis_size("row")
    group = 4
    near = 2
    groups = row_total // group
    cycle_count = src_dev * row_total // (2 * NPH) + 1
    pitch, first_cos, tables = trig_tables(cycle_count)
    sizes = (pitch, first_cos, cycle_count)
    far_total = (groups - 1) * BAND_DEV
    vmem = pl.BlockSpec(memory_space=pltpu.VMEM)
    hbm = pl.BlockSpec(memory_space=pltpu.HBM)
    anywhere = pl.BlockSpec(memory_space=pl.ANY)
    params = pltpu.CompilerParams(vmem_limit_bytes=VMEM)
    def moved(array, target_of):
        return lax.ppermute(array, "row", [(r, target_of(r)) for r in range(row_total)])

    densities = [density, moved(density, lambda r: r ^ 1), moved(density, lambda r: r ^ 2)]

    def shape(*dims, dtype=BF16):
        return jax.ShapeDtypeStruct(dims, dtype)

    def in_hbm(array):
        return pltpu.with_memory_space_constraint(array, pltpu.HBM)

    def cost(sources, targets):
        return pl.CostEstimate(
            flops=2 * sources * targets * 256 * 3, bytes_accessed=1 << 20, transcendentals=0
        )

    small = [lattice_vector.reshape(1, -1), mode_table, *map(jnp.asarray, tables)]
    stage = pltpu.VMEM((2 * min(CHUNK, src_dev) // BLOCK, 8 * FEATS, 128), F32)
    early = far_total - BAND_DEV
    table, origins, tgt_early, tgt_late, tgt_own, part_early, part_late, *near_features, corners = (
        pl.pallas_call(
            lambda *refs: first_kernel(near, row_total, group, sizes, *refs),
            out_shape=[
                shape(pitch, NPH, dtype=F32),
                shape(tables[2].shape[0] + 8, 128, dtype=F32),
                shape(FEATS, early),
                shape(FEATS, BAND_DEV),
                shape(FEATS, BAND_DEV),
                shape(columns, early, dtype=F32),
                shape(columns, BAND_DEV, dtype=F32),
                shape(FEATS, near * src_dev),
                shape(FEATS, near * src_dev),
                shape(3, (group - near) * src_dev, dtype=jnp.int32),
            ],
            in_specs=[pl.BlockSpec(memory_space=pltpu.SMEM)] + [hbm] * 7 + [anywhere] * (near - 1),
            out_specs=[vmem] * 10,
            scratch_shapes=[pltpu.VMEM(array.shape, array.dtype) for array in small]
            + [
                pltpu.VMEM((3, near * src_dev), jnp.int32),
                pltpu.VMEM((3, groups * BAND_DEV), jnp.int32),
                pltpu.VMEM((columns, near * src_dev), BF16),
                stage,
                pltpu.VMEM((FEATS, far_total), BF16),
                pltpu.VMEM((columns, far_total), F32),
                pltpu.SemaphoreType.DMA((5,)),
                pltpu.SemaphoreType.DMA((near,)),
                pltpu.SemaphoreType.DMA((group - near,)),
                pltpu.SemaphoreType.DMA((groups,)),
                pltpu.SemaphoreType.DMA((near,)),
            ],
            compiler_params=params,
            cost_estimate=cost(near * src_dev, far_total),
            name="near_sources",
        )(
            sample_index,
            *[in_hbm(array) for array in (*small, connectivity, density)],
            *densities[1:near],
        )
    )

    relay, origins = lax.optimization_barrier((densities[2], origins))
    densities.append(moved(relay, lambda r: r ^ 1))
    rest = group - near
    *sums, dist_rest, flux_rest = pl.pallas_call(
        lambda *refs: second_kernel(near, group, cycle_count, *refs),
        out_shape=[shape(columns, BAND_DEV)] * (groups - 2)
        + [shape(FEATS, rest * src_dev)] * 2,
        in_specs=[vmem] * 5 + [anywhere] * rest,
        out_specs=[vmem] * groups,
        scratch_shapes=[
            pltpu.VMEM((columns, rest * src_dev), BF16),
            pltpu.VMEM((columns, early), F32),
            stage,
            pltpu.SemaphoreType.DMA((rest,)),
        ],
        compiler_params=params,
        cost_estimate=cost(rest * src_dev, early),
        name="other_sources",
    )(corners, table, origins, tgt_early, part_early, *densities[near:])

    def kept(features, target, blocks, own, part, dtype=F32):
        return pl.pallas_call(
            lambda *refs: kept_kernel(own, len(blocks), *refs),
            out_shape=shape(columns, BAND_DEV, dtype=dtype),
            in_specs=[vmem] * (3 + len(blocks) + len(part)),
            out_specs=vmem,
            compiler_params=params,
            cost_estimate=cost(len(blocks) * src_dev, BAND_DEV),
            name="own_first" if own else "late_targets" if dtype == BF16 else "own_last",
        )(*features, target, *blocks, *part)

    rest_features = (dist_rest, flux_rest)
    own_sums = kept(near_features, tgt_own, densities[:near], True, [])
    sums.append(kept(rest_features, tgt_late, densities[near:], False, [part_late], BF16))
    own_sums = kept(rest_features, tgt_own, densities[near:], False, [own_sums])
    total = 0.5 * density[:, :BAND_DEV].astype(F32) + own_sums
    for k, block in enumerate(sums):
        total = total + moved(
            block, lambda r, k=k: partner(r // group, k + 1, groups) * group + r % group
        ).astype(F32)
    return total.T


def solution(mesh):
    placed = (P("sample"), P(), P(), P(), P(None, "row"))
    return jax.shard_map(
        per_device,
        mesh=mesh,
        in_specs=placed,
        out_specs=P(("sample", "row"), None),
        check_vma=False,
    )
```

```python
import math

import jax
import jax.numpy as jnp
import numpy as np
from jax import lax
from jax.experimental import pallas as pl
from jax.experimental.pallas import tpu as pltpu
from jax.sharding import PartitionSpec as P

NLAT = 32768
NPH = 256
BAND_DEV = 256
FREQS = 32
FEATS = 64
BLOCK = 1024
CHUNK = 1024
TGT_STEP = 768
KEPT_STEP = 1024
VMEM = 30 << 20
F32 = jnp.float32
BF16 = jnp.bfloat16


def split(values):
    first = values.astype(BF16).astype(F32)
    rest = values - first
    second = rest.astype(BF16).astype(F32)
    third = (rest - second).astype(BF16).astype(F32)
    return [first, second, third]


def trig_tables(cycle_count):
    pitch = -(-cycle_count // 8) * 8
    cycle = np.arange(pitch)[:, None]
    polar = np.pi * (cycle + 1.0) / (cycle_count + 1) * (cycle < cycle_count)
    freq = np.arange(FREQS)[None, :]
    polar_table = np.concatenate([np.cos(freq * polar), -np.sin(freq * polar)], axis=0)
    azimuth = 2.0 * np.pi * np.arange(NPH)[None, :] / NPH
    azim_freq = np.arange(FREQS)[:, None] - FREQS // 2
    azim_table = np.concatenate([np.cos(azimuth * azim_freq), np.sin(azimuth * azim_freq)], axis=0)
    rows = -(-cycle_count // 128)
    ring = np.zeros((2, rows * 128))
    ring[0, :cycle_count] = np.sin(polar[:cycle_count, 0])
    ring[1, :cycle_count] = np.cos(polar[:cycle_count, 0])
    angles = np.concatenate(
        [ring.reshape(-1, 128), np.cos(azimuth).reshape(-1, 128), np.sin(azimuth).reshape(-1, 128)]
    )
    angles = np.concatenate([angles, np.zeros((-len(angles) % 8, 128))])
    first_cos = float(np.cos(np.pi / (cycle_count + 1)))
    tables = [polar_table, azim_table, angles]
    return pitch, first_cos, [table.astype(np.float32) for table in tables]


def radius_table(sample, lattice, modes, polar_table, azim_table, pitch):
    shifts = ((sample * lattice) & (NLAT - 1)).astype(F32) / NLAT - 0.5
    polar_freq = modes[0:1, :]
    azim_freq = modes[1:2, :]
    scale = (1 + polar_freq + jnp.abs(azim_freq)).astype(F32)
    coef = 0.8 * shifts / (scale * scale)
    numbers = lax.broadcasted_iota(jnp.int32, (FREQS, modes.shape[1]), 0)
    at_azim = numbers == azim_freq + FREQS // 2
    at_polar = jnp.where(numbers == polar_freq, 1.0, 0.0).astype(BF16)
    grid = None
    for part in split(coef):
        placed = lax.dot_general(
            at_polar,
            jnp.where(at_azim, part, 0.0).astype(BF16),
            (((1,), (1,)), ((), ())),
            preferred_element_type=F32,
        )
        grid = placed if grid is None else grid + placed
    exact = dict(precision=lax.Precision.HIGHEST, preferred_element_type=F32)
    both = jnp.dot(polar_table, grid, **exact)
    return jnp.exp(
        jnp.dot(both[:pitch], azim_table[:FREQS], **exact)
        + jnp.dot(both[pitch:], azim_table[FREQS:], **exact)
    )


def heights(first, last, first_cos):
    found, limits = [], []
    for ring, sign in ((first, first_cos), (last, -first_cos)):
        low = jnp.min(ring, axis=1, keepdims=True) * sign
        high = jnp.max(ring, axis=1, keepdims=True) * sign
        found += [0.25 * low + 0.75 * high, 0.75 * low + 0.25 * high]
        limits.append(0.5 * (low + high))
    return found + limits


def at_lanes(ref, row, first, lanes):
    values = jnp.broadcast_to(ref[row : row + 1, first : first + 128], lanes.shape)
    return jnp.take_along_axis(values, lanes, axis=1)


def radii(table_ref, column, cycles, cycle_count):
    lanes = column & 127
    right = column >= 128
    levels = (cycle_count - 1).bit_length()
    bits = [[(cycle & (1 << level)) != 0 for level in range(levels)] for cycle in cycles]

    def among(low, level):
        if level == 0:
            left = at_lanes(table_ref, low, 0, lanes)
            return [jnp.where(right, at_lanes(table_ref, low, 128, lanes), left)] * len(cycles)
        half = 1 << (level - 1)
        below = among(low, level - 1)
        if low + half >= cycle_count:
            return below
        above = among(low + half, level - 1)
        return [jnp.where(bit[level - 1], y, x) for bit, x, y in zip(bits, below, above)]

    return among(0, levels)


def angle_of(angles_ref, first, rows, index):
    lanes = index & 127
    found = at_lanes(angles_ref, first, 0, lanes)
    for row in range(1, rows):
        found = jnp.where(index >= 128 * row, at_lanes(angles_ref, first + row, 0, lanes), found)
    return found


def panels(corners, table_ref, angles_ref, cycle_count):
    zero, one, two = [
        jnp.concatenate([corners[c : c + 1, k * 128 : (k + 1) * 128] for k in range(8)], axis=0)
        for c in range(3)
    ]
    last = ((zero ^ one) & (NPH - 1)) == 0
    middle = ((zero ^ two) & (NPH - 1)) == 0
    turned = (
        jnp.where(last, two, jnp.where(middle, one, zero)),
        jnp.where(last, zero, jnp.where(middle, two, one)),
        jnp.where(last, one, jnp.where(middle, zero, two)),
    )
    cycles = [corner >> 8 for corner in turned]
    columns = [turned[0] & (NPH - 1), turned[1] & (NPH - 1)]
    radius = radii(table_ref, columns[0], cycles[:1], cycle_count) + radii(
        table_ref, columns[1], cycles[1:], cycle_count
    )
    rows = -(-cycle_count // 128)
    cos = [angle_of(angles_ref, 2 * rows, 2, column) for column in columns]
    sin = [angle_of(angles_ref, 2 * rows + 2, 2, column) for column in columns]
    points = []
    for c in range(3):
        flat = radius[c] * angle_of(angles_ref, 0, rows, cycles[c])
        side = min(c, 1)
        points.append(
            (flat * cos[side], flat * sin[side], radius[c] * angle_of(angles_ref, rows, rows, cycles[c]))
        )
    centers = [(points[0][d] + points[1][d] + points[2][d]) / 3.0 for d in range(3)]
    one = [points[1][d] - points[0][d] for d in range(3)]
    two = [points[2][d] - points[0][d] for d in range(3)]
    half = 0.5 / (4.0 * math.pi)
    areas = [
        half * (one[(d + 1) % 3] * two[(d + 2) % 3] - one[(d + 2) % 3] * two[(d + 1) % 3])
        for d in range(3)
    ]
    return centers, areas


def as_rows(values, stage_ref):
    for k, value in enumerate(values):
        stage_ref[k * 8 : (k + 1) * 8, :] = value
    blocks = [stage_ref[pl.ds(k, len(values), stride=8), :].astype(BF16) for k in range(8)]
    return jnp.concatenate(blocks, axis=1)


def left_pieces(value):
    one, two, three = split(value)
    return [one, one, one, two, two, three]


def right_pieces(value):
    one, two, three = split(value)
    return [one, two, three, one, two, one]


def padded(rows):
    return rows + [jnp.zeros((8, 128), F32)] * (FEATS - len(rows))


def target_features(corners, geometry, stage_ref):
    (x, y, z), _ = panels(corners, *geometry[:3])
    ones = [jnp.ones((8, 128), F32)] * 3
    rows = left_pieces(x) + left_pieces(y) + split(x * x + y * y) + ones
    for height in geometry[3][:4]:
        rise = z - height
        rows += left_pieces(rise) + split(rise * rise)
    return as_rows(padded(rows), stage_ref)


def source_features(corners, geometry, stage_refs):
    (x, y, z), areas = panels(corners, *geometry[:3])
    *levels, north, south = geometry[3]
    upper = z >= 0.0
    places = [z >= north, upper & (z < north), z <= south, ~upper & (z > south)]
    height = jnp.where(
        upper, jnp.where(places[0], levels[0], levels[1]), jnp.where(places[2], levels[2], levels[3])
    )
    rise = z - height
    zeros = jnp.zeros((8, 128), F32)
    square = x * x + y * y + rise * rise
    level = x * areas[0] + y * areas[1] + rise * areas[2]
    found = []
    for (a, b, c), flat, last, stage_ref in (
        ((-2.0 * x, -2.0 * y, -2.0 * rise), zeros + 1.0, square, stage_refs[0]),
        (areas, zeros, -level, stage_refs[1]),
    ):
        rows = right_pieces(a) + right_pieces(b) + [flat] * 3 + split(last)
        along = right_pieces(c) + [flat] * 3
        for place in places:
            rows += [jnp.where(place, row, 0.0) for row in along]
        found.append(as_rows(padded(rows), stage_ref))
    return found


def pair_sums(dist, flux, target, density, apart=None):
    contract = (((0,), (0,)), ((), ()))
    dist_sq = lax.dot_general(dist, target, contract, preferred_element_type=F32)
    flow = lax.dot_general(flux, target, contract, preferred_element_type=F32)
    if apart is not None:
        dist_sq = jnp.concatenate([dist_sq[:BAND_DEV] + apart, dist_sq[BAND_DEV:]], axis=0)
    tile = (flow * lax.rsqrt(dist_sq * dist_sq * dist_sq)).astype(BF16)
    return jnp.dot(density, tile, preferred_element_type=F32)


def far_steps(
    corners_ref, density_refs, target_ref, total_ref, dist_ref, flux_ref, geometry, stage_ref
):
    src_total = corners_ref.shape[1]
    src_dev = density_refs[0].shape[1]
    tgt_total = target_ref.shape[1]
    chunk = min(CHUNK, src_dev)
    steps = src_total // chunk
    tgt_step = max(
        step for step in range(BAND_DEV, TGT_STEP + 1, BAND_DEV) if tgt_total % step == 0
    )
    tgt_steps = tgt_total // tgt_step

    def make(turn):
        here = pl.ds(turn * chunk, chunk)
        corners = corners_ref[:, here]
        blocks = [
            source_features(
                corners[:, k * BLOCK : (k + 1) * BLOCK],
                geometry,
                (stage_ref.at[2 * k], stage_ref.at[2 * k + 1]),
            )
            for k in range(chunk // BLOCK)
        ]
        dist, flux = [jnp.concatenate([block[k] for block in blocks], axis=1) for k in range(2)]
        dist_ref[:, here] = dist
        flux_ref[:, here] = flux
        return dist, flux

    def apply(turn, dist, flux):
        here = pl.ds(turn * chunk, chunk)
        first = turn * chunk % src_dev
        density = density_refs[turn * chunk // src_dev][:, first : first + chunk]

        def some(step):
            cols = pl.ds(pl.multiple_of(step * tgt_step, 128), tgt_step)
            total_ref[:, cols] += pair_sums(dist, flux, target_ref[:, cols], density)

        if tgt_steps == 1:
            some(0)
        else:
            pl.loop(0, tgt_steps)(some)

    kept = make(0)
    for turn in range(steps):
        following = make(turn + 1) if turn + 1 < steps else None
        apply(turn, *kept)
        kept = following


def partner(own, k, groups):
    return own ^ (groups - k) if groups & (groups - 1) == 0 else (own + groups - k) % groups


def start_corners(connectivity_ref, corners_ref, sems, firsts, count):
    copies = []
    for k, first in enumerate(firsts):
        copy = pltpu.make_async_copy(
            connectivity_ref.at[:, pl.ds(pl.multiple_of(first, 128), count)],
            corners_ref.at[:, pl.ds(k * count, count)],
            sems.at[k],
        )
        copy.start()
        copies.append(copy)
    return copies


def first_kernel(near, row_total, group, sizes, sample_ref, *refs):
    small_refs, connectivity_ref, density_refs, refs = refs[:5], refs[5], refs[6 : 6 + near], refs[6 + near :]
    (table_ref, origin_ref, *tgt_refs, dist_ref, flux_ref, rest_ref), refs = refs[:10], refs[10:]
    feature_refs, part_refs = tgt_refs[:3], tgt_refs[3:]
    small, (src_corners, tgt_corners, held_ref, stage_ref, far_ref, total_ref, small_sems, src_sems, rest_sems, tgt_sems, density_sem) = (
        refs[:5], refs[5:],
    )
    lattice_ref, modes_ref, polar_ref, azim_ref, angles_ref = small
    pitch, first_cos, cycle_count = sizes
    src_dev = src_corners.shape[1] // near
    groups = row_total // group
    row = lax.axis_index("row")
    own_group = row // group
    place = row % group
    first_copies = []
    for k in range(5):
        first_copies.append(pltpu.make_async_copy(small_refs[k], small[k], small_sems.at[k]))
        first_copies[k].start()
    copies = start_corners(
        connectivity_ref, tgt_corners, tgt_sems,
        [(partner(own_group, k + 1, groups) * group + place) * src_dev for k in range(groups)], BAND_DEV,
    )
    copies += start_corners(
        connectivity_ref, src_corners, src_sems,
        [(own_group * group + (place ^ k)) * src_dev for k in range(near)], src_dev,
    )
    held_copy = pltpu.make_async_copy(density_refs[0], held_ref, density_sem)
    held_copy.start()
    copies.append(held_copy)
    rest_copies = start_corners(
        connectivity_ref, rest_ref, rest_sems,
        [(own_group * group + (place ^ k)) * src_dev for k in range(near, group)], src_dev,
    )

    for copy in first_copies:
        copy.wait()
    radius = radius_table(
        sample_ref[0], lattice_ref[...], modes_ref[...], polar_ref[...], azim_ref[...], pitch
    )
    rows = angles_ref.shape[0]
    origin_ref[0:rows] = angles_ref[...]
    levels = heights(radius[0:1], radius[cycle_count - 1 : cycle_count], first_cos)
    for k, level in enumerate(levels):
        origin_ref[rows + k : rows + k + 1] = jnp.broadcast_to(level, (1, 128))
    table_ref[...] = radius
    for copy in copies:
        copy.wait()

    geometry = (table_ref, angles_ref, cycle_count, levels)
    found = [
        target_features(tgt_corners[:, first : first + BLOCK], geometry, stage_ref.at[0])
        for first in range(0, tgt_corners.shape[1], BLOCK)
    ]
    found = jnp.concatenate(found, axis=1)
    far_ref[...] = found[:, :-BAND_DEV]
    first = 0
    for ref in feature_refs:
        ref[...] = found[:, first : first + ref.shape[1]]
        first += ref.shape[1]
    total_ref[...] = jnp.zeros_like(total_ref)
    far_steps(
        src_corners,
        (held_ref, *density_refs[1:]),
        far_ref, total_ref, dist_ref, flux_ref, geometry, stage_ref,
    )
    first = 0
    for ref in part_refs:
        ref[...] = total_ref[:, first : first + ref.shape[1]]
        first += ref.shape[1]
    for copy in rest_copies:
        copy.wait()


def second_kernel(
    near, group, cycle_count, corners_ref, table_ref, origin_ref, far_ref, part_ref, *refs
):
    rest = group - near
    density_refs, refs = refs[:rest], refs[rest:]
    (*sums_refs, dist_ref, flux_ref, total_ref, stage_ref) = refs
    rows = origin_ref.shape[0] - 8
    levels = [origin_ref[rows + k : rows + k + 1, 0:1] for k in range(6)]
    geometry = (table_ref, origin_ref, cycle_count, levels)
    total_ref[...] = part_ref[...]
    far_steps(
        corners_ref, density_refs, far_ref, total_ref, dist_ref, flux_ref, geometry, stage_ref
    )
    for k, ref in enumerate(sums_refs):
        ref[...] = total_ref[:, k * BAND_DEV : (k + 1) * BAND_DEV].astype(BF16)


def kept_kernel(own, count, dist_ref, flux_ref, target_ref, *refs):
    density_refs, (*part_refs, sums_ref) = refs[:count], refs[count:]
    src_dev = density_refs[0].shape[1]
    target = target_ref[...]
    apart = None
    if own:
        diagonal = lax.broadcasted_iota(
            jnp.int32, (BAND_DEV, BAND_DEV), 0
        ) == lax.broadcasted_iota(jnp.int32, (BAND_DEV, BAND_DEV), 1)
        apart = jnp.where(diagonal, 1e30, 0.0)
    total = part_refs[0][...] if part_refs else None
    step = KEPT_STEP
    for first in range(0, count * src_dev, step):
        here = slice(first, first + step)
        inside = slice(first % src_dev, first % src_dev + step)
        sums = pair_sums(
            dist_ref[:, here], flux_ref[:, here], target, density_refs[first // src_dev][:, inside],
            None if first else apart,
        )
        total = sums if total is None else total + sums
    sums_ref[...] = total.astype(sums_ref.dtype)


def per_device(sample_index, lattice_vector, mode_table, connectivity, density):
    columns, src_dev = density.shape
    row_total = lax.axis_size("row")
    group = 4
    near = 2
    groups = row_total // group
    cycle_count = src_dev * row_total // (2 * NPH) + 1
    pitch, first_cos, tables = trig_tables(cycle_count)
    sizes = (pitch, first_cos, cycle_count)
    far_total = (groups - 1) * BAND_DEV
    vmem = pl.BlockSpec(memory_space=pltpu.VMEM)
    hbm = pl.BlockSpec(memory_space=pltpu.HBM)
    params = pltpu.CompilerParams(vmem_limit_bytes=VMEM)
    def moved(array, target_of):
        return lax.ppermute(array, "row", [(r, target_of(r)) for r in range(row_total)])

    densities = [density, moved(density, lambda r: r ^ 1), moved(density, lambda r: r ^ 2)]

    def shape(*dims, dtype=BF16):
        return jax.ShapeDtypeStruct(dims, dtype)

    def in_hbm(array):
        return pltpu.with_memory_space_constraint(array, pltpu.HBM)

    def cost(sources, targets):
        return pl.CostEstimate(
            flops=2 * sources * targets * 256 * 3, bytes_accessed=1 << 20, transcendentals=0
        )

    small = [lattice_vector.reshape(1, -1), mode_table, *map(jnp.asarray, tables)]
    stage = pltpu.VMEM((2 * min(CHUNK, src_dev) // BLOCK, 8 * FEATS, 128), F32)
    early = far_total - BAND_DEV
    table, origins, tgt_early, tgt_late, tgt_own, part_early, part_late, *near_features, corners = (
        pl.pallas_call(
            lambda *refs: first_kernel(near, row_total, group, sizes, *refs),
            out_shape=[
                shape(pitch, NPH, dtype=F32),
                shape(tables[2].shape[0] + 8, 128, dtype=F32),
                shape(FEATS, early),
                shape(FEATS, BAND_DEV),
                shape(FEATS, BAND_DEV),
                shape(columns, early, dtype=F32),
                shape(columns, BAND_DEV, dtype=F32),
                shape(FEATS, near * src_dev),
                shape(FEATS, near * src_dev),
                shape(3, (group - near) * src_dev, dtype=jnp.int32),
            ],
            in_specs=[pl.BlockSpec(memory_space=pltpu.SMEM)] + [hbm] * 7 + [vmem] * (near - 1),
            out_specs=[vmem] * 10,
            scratch_shapes=[pltpu.VMEM(array.shape, array.dtype) for array in small]
            + [
                pltpu.VMEM((3, near * src_dev), jnp.int32),
                pltpu.VMEM((3, groups * BAND_DEV), jnp.int32),
                pltpu.VMEM((columns, src_dev), BF16),
                stage,
                pltpu.VMEM((FEATS, far_total), BF16),
                pltpu.VMEM((columns, far_total), F32),
                pltpu.SemaphoreType.DMA((5,)),
                pltpu.SemaphoreType.DMA((near,)),
                pltpu.SemaphoreType.DMA((group - near,)),
                pltpu.SemaphoreType.DMA((groups,)),
                pltpu.SemaphoreType.DMA,
            ],
            compiler_params=params,
            cost_estimate=cost(near * src_dev, far_total),
            name="near_sources",
        )(
            sample_index,
            *[in_hbm(array) for array in (*small, connectivity, density)],
            *densities[1:near],
        )
    )

    relay, origins = lax.optimization_barrier((densities[2], origins))
    densities.append(moved(relay, lambda r: r ^ 1))
    rest = group - near
    *sums, dist_rest, flux_rest = pl.pallas_call(
        lambda *refs: second_kernel(near, group, cycle_count, *refs),
        out_shape=[shape(columns, BAND_DEV)] * (groups - 2)
        + [shape(FEATS, rest * src_dev)] * 2,
        in_specs=[vmem] * (5 + rest),
        out_specs=[vmem] * groups,
        scratch_shapes=[
            pltpu.VMEM((columns, early), F32),
            stage,
        ],
        compiler_params=params,
        cost_estimate=cost(rest * src_dev, early),
        name="other_sources",
    )(corners, table, origins, tgt_early, part_early, *densities[near:])

    def kept(features, target, blocks, own, part, dtype=F32):
        return pl.pallas_call(
            lambda *refs: kept_kernel(own, len(blocks), *refs),
            out_shape=shape(columns, BAND_DEV, dtype=dtype),
            in_specs=[vmem] * (3 + len(blocks) + len(part)),
            out_specs=vmem,
            compiler_params=params,
            cost_estimate=cost(len(blocks) * src_dev, BAND_DEV),
            name="own_first" if own else "late_targets" if dtype == BF16 else "own_last",
        )(*features, target, *blocks, *part)

    rest_features = (dist_rest, flux_rest)
    own_sums = kept(near_features, tgt_own, densities[:near], True, [])
    sums.append(kept(rest_features, tgt_late, densities[near:], False, [part_late], BF16))
    own_sums = kept(rest_features, tgt_own, densities[near:], False, [own_sums])
    total = 0.5 * density[:, :BAND_DEV].astype(F32) + own_sums
    for k, block in enumerate(sums):
        total = total + moved(
            block, lambda r, k=k: partner(r // group, k + 1, groups) * group + r % group
        ).astype(F32)
    return total.T


def solution(mesh):
    placed = (P("sample"), P(), P(), P(), P(None, "row"))
    return jax.shard_map(
        per_device,
        mesh=mesh,
        in_specs=placed,
        out_specs=P(("sample", "row"), None),
        check_vma=False,
    )
```

```python
import math

import jax
import jax.numpy as jnp
import numpy as np
from jax import lax
from jax.experimental import pallas as pl
from jax.experimental.pallas import tpu as pltpu
from jax.sharding import PartitionSpec as P

NLAT = 32768
NPH = 256
BAND_DEV = 256
FREQS = 32
FEATS = 64
BLOCK = 1024
CHUNK = 1024
TGT_STEP = 768
KEPT_STEP = 1024
VMEM = 30 << 20
F32 = jnp.float32
BF16 = jnp.bfloat16


def split(values):
    first = values.astype(BF16).astype(F32)
    rest = values - first
    second = rest.astype(BF16).astype(F32)
    third = (rest - second).astype(BF16).astype(F32)
    return [first, second, third]


def trig_tables(cycle_count):
    pitch = -(-cycle_count // 8) * 8
    cycle = np.arange(pitch)[:, None]
    polar = np.pi * (cycle + 1.0) / (cycle_count + 1) * (cycle < cycle_count)
    freq = np.arange(FREQS)[None, :]
    polar_table = np.concatenate([np.cos(freq * polar), -np.sin(freq * polar)], axis=0)
    azimuth = 2.0 * np.pi * np.arange(NPH)[None, :] / NPH
    azim_freq = np.arange(FREQS)[:, None] - FREQS // 2
    azim_table = np.concatenate([np.cos(azimuth * azim_freq), np.sin(azimuth * azim_freq)], axis=0)
    rows = -(-cycle_count // 128)
    ring = np.zeros((2, rows * 128))
    ring[0, :cycle_count] = np.sin(polar[:cycle_count, 0])
    ring[1, :cycle_count] = np.cos(polar[:cycle_count, 0])
    angles = np.concatenate(
        [ring.reshape(-1, 128), np.cos(azimuth).reshape(-1, 128), np.sin(azimuth).reshape(-1, 128)]
    )
    angles = np.concatenate([angles, np.zeros((-len(angles) % 8, 128))])
    first_cos = float(np.cos(np.pi / (cycle_count + 1)))
    tables = [polar_table, azim_table, angles]
    return pitch, first_cos, [table.astype(np.float32) for table in tables]


def radius_table(sample, lattice, modes, polar_table, azim_table, pitch):
    shifts = ((sample * lattice) & (NLAT - 1)).astype(F32) / NLAT - 0.5
    polar_freq = modes[0:1, :]
    azim_freq = modes[1:2, :]
    scale = (1 + polar_freq + jnp.abs(azim_freq)).astype(F32)
    coef = 0.8 * shifts / (scale * scale)
    numbers = lax.broadcasted_iota(jnp.int32, (FREQS, modes.shape[1]), 0)
    at_azim = numbers == azim_freq + FREQS // 2
    at_polar = jnp.where(numbers == polar_freq, 1.0, 0.0).astype(BF16)
    grid = None
    for part in split(coef):
        placed = lax.dot_general(
            at_polar,
            jnp.where(at_azim, part, 0.0).astype(BF16),
            (((1,), (1,)), ((), ())),
            preferred_element_type=F32,
        )
        grid = placed if grid is None else grid + placed
    exact = dict(precision=lax.Precision.HIGHEST, preferred_element_type=F32)
    both = jnp.dot(polar_table, grid, **exact)
    return jnp.exp(
        jnp.dot(both[:pitch], azim_table[:FREQS], **exact)
        + jnp.dot(both[pitch:], azim_table[FREQS:], **exact)
    )


def heights(first, last, first_cos):
    found, limits = [], []
    for ring, sign in ((first, first_cos), (last, -first_cos)):
        low = jnp.min(ring, axis=1, keepdims=True) * sign
        high = jnp.max(ring, axis=1, keepdims=True) * sign
        found += [0.25 * low + 0.75 * high, 0.75 * low + 0.25 * high]
        limits.append(0.5 * (low + high))
    return found + limits


def at_lanes(ref, row, first, lanes):
    values = jnp.broadcast_to(ref[row : row + 1, first : first + 128], lanes.shape)
    return jnp.take_along_axis(values, lanes, axis=1)


def radii(table_ref, column, cycles, cycle_count):
    lanes = column & 127
    right = column >= 128
    levels = (cycle_count - 1).bit_length()
    bits = [[(cycle & (1 << level)) != 0 for level in range(levels)] for cycle in cycles]

    def among(low, level):
        if level == 0:
            left = at_lanes(table_ref, low, 0, lanes)
            return [jnp.where(right, at_lanes(table_ref, low, 128, lanes), left)] * len(cycles)
        half = 1 << (level - 1)
        below = among(low, level - 1)
        if low + half >= cycle_count:
            return below
        above = among(low + half, level - 1)
        return [jnp.where(bit[level - 1], y, x) for bit, x, y in zip(bits, below, above)]

    return among(0, levels)


def angle_of(angles_ref, first, rows, index):
    lanes = index & 127
    found = at_lanes(angles_ref, first, 0, lanes)
    for row in range(1, rows):
        found = jnp.where(index >= 128 * row, at_lanes(angles_ref, first + row, 0, lanes), found)
    return found


def panels(corners, table_ref, angles_ref, cycle_count):
    zero, one, two = [
        jnp.concatenate([corners[c : c + 1, k * 128 : (k + 1) * 128] for k in range(8)], axis=0)
        for c in range(3)
    ]
    last = ((zero ^ one) & (NPH - 1)) == 0
    middle = ((zero ^ two) & (NPH - 1)) == 0
    turned = (
        jnp.where(last, two, jnp.where(middle, one, zero)),
        jnp.where(last, zero, jnp.where(middle, two, one)),
        jnp.where(last, one, jnp.where(middle, zero, two)),
    )
    cycles = [corner >> 8 for corner in turned]
    columns = [turned[0] & (NPH - 1), turned[1] & (NPH - 1)]
    radius = radii(table_ref, columns[0], cycles[:1], cycle_count) + radii(
        table_ref, columns[1], cycles[1:], cycle_count
    )
    rows = -(-cycle_count // 128)
    cos = [angle_of(angles_ref, 2 * rows, 2, column) for column in columns]
    sin = [angle_of(angles_ref, 2 * rows + 2, 2, column) for column in columns]
    points = []
    for c in range(3):
        flat = radius[c] * angle_of(angles_ref, 0, rows, cycles[c])
        side = min(c, 1)
        points.append(
            (flat * cos[side], flat * sin[side], radius[c] * angle_of(angles_ref, rows, rows, cycles[c]))
        )
    centers = [(points[0][d] + points[1][d] + points[2][d]) / 3.0 for d in range(3)]
    one = [points[1][d] - points[0][d] for d in range(3)]
    two = [points[2][d] - points[0][d] for d in range(3)]
    half = 0.5 / (4.0 * math.pi)
    areas = [
        half * (one[(d + 1) % 3] * two[(d + 2) % 3] - one[(d + 2) % 3] * two[(d + 1) % 3])
        for d in range(3)
    ]
    return centers, areas


def as_rows(values, stage_ref):
    for k, value in enumerate(values):
        stage_ref[k * 8 : (k + 1) * 8, :] = value
    blocks = [stage_ref[pl.ds(k, len(values), stride=8), :].astype(BF16) for k in range(8)]
    return jnp.concatenate(blocks, axis=1)


def left_pieces(value):
    one, two, three = split(value)
    return [one, one, one, two, two, three]


def right_pieces(value):
    one, two, three = split(value)
    return [one, two, three, one, two, one]


def padded(rows):
    return rows + [jnp.zeros((8, 128), F32)] * (FEATS - len(rows))


def target_features(corners, geometry, stage_ref):
    (x, y, z), _ = panels(corners, *geometry[:3])
    ones = [jnp.ones((8, 128), F32)] * 3
    rows = left_pieces(x) + left_pieces(y) + split(x * x + y * y) + ones
    for height in geometry[3][:4]:
        rise = z - height
        rows += left_pieces(rise) + split(rise * rise)
    return as_rows(padded(rows), stage_ref)


def source_features(corners, geometry, stage_refs):
    (x, y, z), areas = panels(corners, *geometry[:3])
    *levels, north, south = geometry[3]
    upper = z >= 0.0
    places = [z >= north, upper & (z < north), z <= south, ~upper & (z > south)]
    height = jnp.where(
        upper, jnp.where(places[0], levels[0], levels[1]), jnp.where(places[2], levels[2], levels[3])
    )
    rise = z - height
    zeros = jnp.zeros((8, 128), F32)
    square = x * x + y * y + rise * rise
    level = x * areas[0] + y * areas[1] + rise * areas[2]
    found = []
    for (a, b, c), flat, last, stage_ref in (
        ((-2.0 * x, -2.0 * y, -2.0 * rise), zeros + 1.0, square, stage_refs[0]),
        (areas, zeros, -level, stage_refs[1]),
    ):
        rows = right_pieces(a) + right_pieces(b) + [flat] * 3 + split(last)
        along = right_pieces(c) + [flat] * 3
        for place in places:
            rows += [jnp.where(place, row, 0.0) for row in along]
        found.append(as_rows(padded(rows), stage_ref))
    return found


def pair_sums(dist, flux, target, density, apart=None):
    contract = (((0,), (0,)), ((), ()))
    dist_sq = lax.dot_general(dist, target, contract, preferred_element_type=F32)
    flow = lax.dot_general(flux, target, contract, preferred_element_type=F32)
    if apart is not None:
        dist_sq = jnp.concatenate([dist_sq[:BAND_DEV] + apart, dist_sq[BAND_DEV:]], axis=0)
    tile = (flow * lax.rsqrt(dist_sq * dist_sq * dist_sq)).astype(BF16)
    return jnp.dot(density, tile, preferred_element_type=F32)


def chunk_features(corners, geometry, stage_ref):
    blocks = [
        source_features(
            corners[:, k * BLOCK : (k + 1) * BLOCK],
            geometry,
            (stage_ref.at[2 * k], stage_ref.at[2 * k + 1]),
        )
        for k in range(corners.shape[1] // BLOCK)
    ]
    return [jnp.concatenate([block[k] for block in blocks], axis=1) for k in range(2)]


def source_steps(
    corners_ref, first, density_refs, target_ref, total_ref, ready_refs, kept_refs, next_refs,
    geometry, stage_ref,
):
    src_dev = density_refs[0].shape[1]
    src_total = src_dev * len(density_refs)
    tgt_total = total_ref.shape[1]
    chunk = min(CHUNK, src_dev)
    steps = src_total // chunk
    tgt_step = max(
        step for step in range(BAND_DEV, TGT_STEP + 1, BAND_DEV) if tgt_total % step == 0
    )
    tgt_steps = tgt_total // tgt_step

    def make(turn):
        start = first * src_dev + turn * chunk
        return chunk_features(corners_ref[:, start : start + chunk], geometry, stage_ref)

    def apply(turn, dist, flux):
        here = pl.ds(turn * chunk, chunk)
        first = turn * chunk % src_dev
        density = density_refs[turn * chunk // src_dev][:, first : first + chunk]

        def some(step):
            cols = pl.ds(pl.multiple_of(step * tgt_step, 128), tgt_step)
            total_ref[:, cols] += pair_sums(dist, flux, target_ref[:, cols], density)

        if tgt_steps == 1:
            some(0)
        else:
            pl.loop(0, tgt_steps)(some)

    kept = [ref[...] for ref in ready_refs] if ready_refs else make(0)
    for turn in range(steps):
        for ref, values in zip(kept_refs, kept):
            ref[:, turn * chunk : (turn + 1) * chunk] = values
        following = make(turn + 1) if turn + 1 < steps or next_refs else None
        apply(turn, *kept)
        kept = following
    for ref, values in zip(next_refs, kept or ()):
        ref[...] = values


def partner(own, k, groups):
    return own ^ (groups - k) if groups & (groups - 1) == 0 else (own + groups - k) % groups


def start_corners(connectivity_ref, corners_ref, sems, firsts, count):
    copies = []
    for k, first in enumerate(firsts):
        copy = pltpu.make_async_copy(
            connectivity_ref.at[:, pl.ds(pl.multiple_of(first, 128), count)],
            corners_ref.at[:, pl.ds(k * count, count)],
            sems.at[k],
        )
        copy.start()
        copies.append(copy)
    return copies


def prepare_kernel(row_total, group, sizes, sample_ref, *refs):
    small_refs, connectivity_ref, refs = refs[:5], refs[5], refs[6:]
    (table_ref, origin_ref, far_ref, own_ref, src_corners), refs = refs[:5], refs[5:]
    small, (tgt_corners, tgt_stage_ref, stage_ref, small_sems, src_sems, tgt_sems) = refs[:5], refs[5:]
    lattice_ref, modes_ref, polar_ref, azim_ref, angles_ref = small
    pitch, first_cos, cycle_count = sizes
    src_dev = src_corners.shape[1] // group
    groups = row_total // group
    row = lax.axis_index("row")
    own_group = row // group
    place = row % group
    small_copies = []
    for k in range(5):
        small_copies.append(pltpu.make_async_copy(small_refs[k], small[k], small_sems.at[k]))
        small_copies[k].start()
    tgt_copies = start_corners(
        connectivity_ref, tgt_corners, tgt_sems,
        [(partner(own_group, k + 1, groups) * group + place) * src_dev for k in range(groups)], BAND_DEV,
    )
    src_copies = start_corners(
        connectivity_ref, src_corners, src_sems,
        [(own_group * group + (place ^ k)) * src_dev for k in range(group)], src_dev,
    )
    for copy in small_copies:
        copy.wait()
    radius = radius_table(
        sample_ref[0], lattice_ref[...], modes_ref[...], polar_ref[...], azim_ref[...], pitch
    )
    rows = angles_ref.shape[0]
    origin_ref[0:rows] = angles_ref[...]
    levels = heights(radius[0:1], radius[cycle_count - 1 : cycle_count], first_cos)
    for k, level in enumerate(levels):
        origin_ref[rows + k : rows + k + 1] = jnp.broadcast_to(level, (1, 128))
    table_ref[...] = radius
    for copy in tgt_copies + src_copies:
        copy.wait()
    geometry = (table_ref, angles_ref, cycle_count, levels)
    found = [
        target_features(tgt_corners[:, first : first + BLOCK], geometry, tgt_stage_ref)
        for first in range(0, tgt_corners.shape[1], BLOCK)
    ]
    found = jnp.concatenate(found, axis=1)
    far_ref[...] = found[:, :-BAND_DEV]
    own_ref[...] = found[:, -BAND_DEV:]


def sources_kernel(first, count, cycle_count, corners_ref, table_ref, origin_ref, far_ref, *refs):
    ready_refs, refs = (refs[:2], refs[2:]) if first else ((), refs)
    part_refs, refs = (refs[:1], refs[1:]) if first else ((), refs)
    density_refs, (*sums_refs, total_ref, stage_ref) = refs[:count], refs[count:]
    sums_refs, next_refs = (sums_refs, ()) if first else (sums_refs[:-2], sums_refs[-2:])
    sums_refs, kept_refs = sums_refs[:-2], sums_refs[-2:]
    rows = origin_ref.shape[0] - 8
    levels = [origin_ref[rows + k : rows + k + 1, 0:1] for k in range(6)]
    geometry = (table_ref, origin_ref, cycle_count, levels)
    if part_refs:
        total_ref[...] = part_refs[0][:, : total_ref.shape[1]]
    else:
        total_ref[...] = jnp.zeros_like(total_ref)
    source_steps(
        corners_ref, first, density_refs, far_ref, total_ref, ready_refs, kept_refs, next_refs,
        geometry, stage_ref,
    )
    width = sums_refs[0].shape[1]
    for k, ref in enumerate(sums_refs):
        ref[...] = total_ref[:, k * width : (k + 1) * width].astype(ref.dtype)


def kept_kernel(own, count, dist_ref, flux_ref, target_ref, *refs):
    density_refs, (*part_refs, sums_ref) = refs[:count], refs[count:]
    src_dev = density_refs[0].shape[1]
    target = target_ref[:, -BAND_DEV:]
    apart = None
    if own:
        diagonal = lax.broadcasted_iota(
            jnp.int32, (BAND_DEV, BAND_DEV), 0
        ) == lax.broadcasted_iota(jnp.int32, (BAND_DEV, BAND_DEV), 1)
        apart = jnp.where(diagonal, 1e30, 0.0)
    total = part_refs[0][:, -BAND_DEV:] if part_refs else None
    step = KEPT_STEP
    for first in range(0, count * src_dev, step):
        here = slice(first, first + step)
        inside = slice(first % src_dev, first % src_dev + step)
        sums = pair_sums(
            dist_ref[:, here], flux_ref[:, here], target, density_refs[first // src_dev][:, inside],
            None if first else apart,
        )
        total = sums if total is None else total + sums
    sums_ref[...] = total.astype(sums_ref.dtype)


def per_device(sample_index, lattice_vector, mode_table, connectivity, density):
    columns, src_dev = density.shape
    row_total = lax.axis_size("row")
    group = 4
    near = 2
    groups = row_total // group
    cycle_count = src_dev * row_total // (2 * NPH) + 1
    pitch, first_cos, tables = trig_tables(cycle_count)
    sizes = (pitch, first_cos, cycle_count)
    far_total = (groups - 1) * BAND_DEV
    vmem = pl.BlockSpec(memory_space=pltpu.VMEM)
    hbm = pl.BlockSpec(memory_space=pltpu.HBM)
    params = pltpu.CompilerParams(vmem_limit_bytes=VMEM)
    def moved(array, target_of):
        return lax.ppermute(array, "row", [(r, target_of(r)) for r in range(row_total)])

    densities = [density, moved(density, lambda r: r ^ 1), moved(density, lambda r: r ^ 2)]

    def shape(*dims, dtype=BF16):
        return jax.ShapeDtypeStruct(dims, dtype)

    def in_hbm(array):
        return pltpu.with_memory_space_constraint(array, pltpu.HBM)

    def cost(sources, targets):
        return pl.CostEstimate(
            flops=2 * sources * targets * 256 * 3, bytes_accessed=1 << 20, transcendentals=0
        )

    small = [lattice_vector.reshape(1, -1), mode_table, *map(jnp.asarray, tables)]
    stage = pltpu.VMEM((2 * min(CHUNK, src_dev) // BLOCK, 8 * FEATS, 128), F32)
    ready_shapes = [shape(FEATS, min(CHUNK, src_dev))] * 2
    table, origins, tgt_far, tgt_own, corners = pl.pallas_call(
        lambda *refs: prepare_kernel(row_total, group, sizes, *refs),
        out_shape=[
            shape(pitch, NPH, dtype=F32),
            shape(tables[2].shape[0] + 8, 128, dtype=F32),
            shape(FEATS, far_total),
            shape(FEATS, BAND_DEV),
            shape(3, group * src_dev, dtype=jnp.int32),
        ],
        in_specs=[pl.BlockSpec(memory_space=pltpu.SMEM)] + [hbm] * 6,
        out_specs=[vmem] * 5,
        scratch_shapes=[pltpu.VMEM(array.shape, array.dtype) for array in small]
        + [
            pltpu.VMEM((3, groups * BAND_DEV), jnp.int32),
            pltpu.VMEM((8 * FEATS, 128), F32),
            stage,
            pltpu.SemaphoreType.DMA((5,)),
            pltpu.SemaphoreType.DMA((group,)),
            pltpu.SemaphoreType.DMA((groups,)),
        ],
        compiler_params=params,
        cost_estimate=cost(1024, 256),
        name="prepare",
    )(sample_index, *[in_hbm(array) for array in (*small, connectivity)])

    def sources(first, blocks, ready, part, total, sums):
        handed_on = [] if first else ready_shapes
        *sums, dist, flux = pl.pallas_call(
            lambda *refs: sources_kernel(first, len(blocks), cycle_count, *refs),
            out_shape=sums + [shape(FEATS, len(blocks) * src_dev)] * 2 + handed_on,
            in_specs=[vmem] * (4 + len(ready) + len(part) + len(blocks)),
            out_specs=[vmem] * (len(sums) + 2 + len(handed_on)),
            scratch_shapes=[pltpu.VMEM((columns, total), F32), stage],
            compiler_params=params,
            cost_estimate=cost(len(blocks) * src_dev, total),
            name="other_sources" if first else "near_sources",
        )(corners, table, origins, tgt_far, *ready, *part, *blocks)
        return sums, (dist, flux)

    early = far_total - BAND_DEV
    (part, *near_features), ready = sources(
        0, densities[:near], [], [], far_total, [shape(columns, far_total, dtype=F32)]
    )
    relay, part = lax.optimization_barrier((densities[2], part))
    densities.append(moved(relay, lambda r: r ^ 1))
    sums, rest_features = sources(
        near, densities[near:], ready, [part], early, [shape(columns, BAND_DEV)] * (groups - 2)
    )

    def kept(features, target, blocks, own, part, dtype=F32):
        return pl.pallas_call(
            lambda *refs: kept_kernel(own, len(blocks), *refs),
            out_shape=shape(columns, BAND_DEV, dtype=dtype),
            in_specs=[vmem] * (3 + len(blocks) + len(part)),
            out_specs=vmem,
            compiler_params=params,
            cost_estimate=cost(len(blocks) * src_dev, BAND_DEV),
            name="own_first" if own else "late_targets" if dtype == BF16 else "own_last",
        )(*features, target, *blocks, *part)

    own_sums = kept(near_features, tgt_own, densities[:near], True, [])
    sums.append(kept(rest_features, tgt_far, densities[near:], False, [part], BF16))
    own_sums = kept(rest_features, tgt_own, densities[near:], False, [own_sums])
    total = 0.5 * density[:, :BAND_DEV].astype(F32) + own_sums
    for k, block in enumerate(sums):
        total = total + moved(
            block, lambda r, k=k: partner(r // group, k + 1, groups) * group + r % group
        ).astype(F32)
    return total.T


def solution(mesh):
    placed = (P("sample"), P(), P(), P(), P(None, "row"))
    return jax.shard_map(
        per_device,
        mesh=mesh,
        in_specs=placed,
        out_specs=P(("sample", "row"), None),
        check_vma=False,
    )
```

```python
import math

import jax
import jax.numpy as jnp
import numpy as np
from jax import lax
from jax.experimental import pallas as pl
from jax.experimental.pallas import tpu as pltpu
from jax.sharding import PartitionSpec as P

NLAT = 32768
NPH = 256
BAND_DEV = 256
FREQS = 32
FEATS = 64
BLOCK = 1024
CHUNK = 1024
TGT_STEP = 768
KEPT_STEP = 1024
VMEM = 40 << 20
F32 = jnp.float32
BF16 = jnp.bfloat16


def split(values):
    first = values.astype(BF16).astype(F32)
    rest = values - first
    second = rest.astype(BF16).astype(F32)
    third = (rest - second).astype(BF16).astype(F32)
    return [first, second, third]


def trig_tables(cycle_count):
    pitch = -(-cycle_count // 8) * 8
    cycle = np.arange(pitch)[:, None]
    polar = np.pi * (cycle + 1.0) / (cycle_count + 1) * (cycle < cycle_count)
    freq = np.arange(FREQS)[None, :]
    polar_table = np.concatenate([np.cos(freq * polar), -np.sin(freq * polar)], axis=0)
    azimuth = 2.0 * np.pi * np.arange(NPH)[None, :] / NPH
    azim_freq = np.arange(FREQS)[:, None] - FREQS // 2
    azim_table = np.concatenate([np.cos(azimuth * azim_freq), np.sin(azimuth * azim_freq)], axis=0)
    rows = -(-cycle_count // 128)
    ring = np.zeros((2, rows * 128))
    ring[0, :cycle_count] = np.sin(polar[:cycle_count, 0])
    ring[1, :cycle_count] = np.cos(polar[:cycle_count, 0])
    angles = np.concatenate(
        [ring.reshape(-1, 128), np.cos(azimuth).reshape(-1, 128), np.sin(azimuth).reshape(-1, 128)]
    )
    angles = np.concatenate([angles, np.zeros((-len(angles) % 8, 128))])
    first_cos = float(np.cos(np.pi / (cycle_count + 1)))
    tables = [polar_table, azim_table, angles]
    return pitch, first_cos, [table.astype(np.float32) for table in tables]


def radius_table(sample, lattice, modes, polar_table, azim_table, pitch):
    shifts = ((sample * lattice) & (NLAT - 1)).astype(F32) / NLAT - 0.5
    polar_freq = modes[0:1, :]
    azim_freq = modes[1:2, :]
    scale = (1 + polar_freq + jnp.abs(azim_freq)).astype(F32)
    coef = 0.8 * shifts / (scale * scale)
    numbers = lax.broadcasted_iota(jnp.int32, (FREQS, modes.shape[1]), 0)
    at_azim = numbers == azim_freq + FREQS // 2
    at_polar = jnp.where(numbers == polar_freq, 1.0, 0.0).astype(BF16)
    grid = None
    for part in split(coef):
        placed = lax.dot_general(
            at_polar,
            jnp.where(at_azim, part, 0.0).astype(BF16),
            (((1,), (1,)), ((), ())),
            preferred_element_type=F32,
        )
        grid = placed if grid is None else grid + placed
    exact = dict(precision=lax.Precision.HIGHEST, preferred_element_type=F32)
    both = jnp.dot(polar_table, grid, **exact)
    return jnp.exp(
        jnp.dot(both[:pitch], azim_table[:FREQS], **exact)
        + jnp.dot(both[pitch:], azim_table[FREQS:], **exact)
    )


def heights(first, last, first_cos):
    found, limits = [], []
    for ring, sign in ((first, first_cos), (last, -first_cos)):
        low = jnp.min(ring, axis=1, keepdims=True) * sign
        high = jnp.max(ring, axis=1, keepdims=True) * sign
        found += [0.25 * low + 0.75 * high, 0.75 * low + 0.25 * high]
        limits.append(0.5 * (low + high))
    return found + limits


def at_lanes(ref, row, first, lanes):
    values = jnp.broadcast_to(ref[row : row + 1, first : first + 128], lanes.shape)
    return jnp.take_along_axis(values, lanes, axis=1)


def radii(table_ref, column, cycles, cycle_count):
    lanes = column & 127
    right = column >= 128
    levels = (cycle_count - 1).bit_length()
    bits = [[(cycle & (1 << level)) != 0 for level in range(levels)] for cycle in cycles]

    def among(low, level):
        if level == 0:
            left = at_lanes(table_ref, low, 0, lanes)
            return [jnp.where(right, at_lanes(table_ref, low, 128, lanes), left)] * len(cycles)
        half = 1 << (level - 1)
        below = among(low, level - 1)
        if low + half >= cycle_count:
            return below
        above = among(low + half, level - 1)
        return [jnp.where(bit[level - 1], y, x) for bit, x, y in zip(bits, below, above)]

    return among(0, levels)


def angle_of(angles_ref, first, rows, index):
    lanes = index & 127
    found = at_lanes(angles_ref, first, 0, lanes)
    for row in range(1, rows):
        found = jnp.where(index >= 128 * row, at_lanes(angles_ref, first + row, 0, lanes), found)
    return found


def panels(corners, table_ref, angles_ref, cycle_count):
    zero, one, two = [
        jnp.concatenate([corners[c : c + 1, k * 128 : (k + 1) * 128] for k in range(8)], axis=0)
        for c in range(3)
    ]
    last = ((zero ^ one) & (NPH - 1)) == 0
    middle = ((zero ^ two) & (NPH - 1)) == 0
    turned = (
        jnp.where(last, two, jnp.where(middle, one, zero)),
        jnp.where(last, zero, jnp.where(middle, two, one)),
        jnp.where(last, one, jnp.where(middle, zero, two)),
    )
    cycles = [corner >> 8 for corner in turned]
    columns = [turned[0] & (NPH - 1), turned[1] & (NPH - 1)]
    radius = radii(table_ref, columns[0], cycles[:1], cycle_count) + radii(
        table_ref, columns[1], cycles[1:], cycle_count
    )
    rows = -(-cycle_count // 128)
    cos = [angle_of(angles_ref, 2 * rows, 2, column) for column in columns]
    sin = [angle_of(angles_ref, 2 * rows + 2, 2, column) for column in columns]
    points = []
    for c in range(3):
        flat = radius[c] * angle_of(angles_ref, 0, rows, cycles[c])
        side = min(c, 1)
        points.append(
            (flat * cos[side], flat * sin[side], radius[c] * angle_of(angles_ref, rows, rows, cycles[c]))
        )
    centers = [(points[0][d] + points[1][d] + points[2][d]) / 3.0 for d in range(3)]
    one = [points[1][d] - points[0][d] for d in range(3)]
    two = [points[2][d] - points[0][d] for d in range(3)]
    half = 0.5 / (4.0 * math.pi)
    areas = [
        half * (one[(d + 1) % 3] * two[(d + 2) % 3] - one[(d + 2) % 3] * two[(d + 1) % 3])
        for d in range(3)
    ]
    return centers, areas


def as_rows(values, stage_ref):
    for k, value in enumerate(values):
        stage_ref[k * 8 : (k + 1) * 8, :] = value
    blocks = [stage_ref[pl.ds(k, len(values), stride=8), :].astype(BF16) for k in range(8)]
    return jnp.concatenate(blocks, axis=1)


def left_pieces(value):
    one, two, three = split(value)
    return [one, one, one, two, two, three]


def right_pieces(value):
    one, two, three = split(value)
    return [one, two, three, one, two, one]


def padded(rows):
    return rows + [jnp.zeros((8, 128), F32)] * (FEATS - len(rows))


def target_features(corners, geometry, stage_ref):
    (x, y, z), _ = panels(corners, *geometry[:3])
    ones = [jnp.ones((8, 128), F32)] * 3
    rows = left_pieces(x) + left_pieces(y) + split(x * x + y * y) + ones
    for height in geometry[3][:4]:
        rise = z - height
        rows += left_pieces(rise) + split(rise * rise)
    return as_rows(padded(rows), stage_ref)


def source_features(corners, geometry, stage_refs):
    (x, y, z), areas = panels(corners, *geometry[:3])
    *levels, north, south = geometry[3]
    upper = z >= 0.0
    places = [z >= north, upper & (z < north), z <= south, ~upper & (z > south)]
    height = jnp.where(
        upper, jnp.where(places[0], levels[0], levels[1]), jnp.where(places[2], levels[2], levels[3])
    )
    rise = z - height
    zeros = jnp.zeros((8, 128), F32)
    square = x * x + y * y + rise * rise
    level = x * areas[0] + y * areas[1] + rise * areas[2]
    found = []
    for (a, b, c), flat, last, stage_ref in (
        ((-2.0 * x, -2.0 * y, -2.0 * rise), zeros + 1.0, square, stage_refs[0]),
        (areas, zeros, -level, stage_refs[1]),
    ):
        rows = right_pieces(a) + right_pieces(b) + [flat] * 3 + split(last)
        along = right_pieces(c) + [flat] * 3
        for place in places:
            rows += [jnp.where(place, row, 0.0) for row in along]
        found.append(as_rows(padded(rows), stage_ref))
    return found


def pair_sums(dist, flux, target, density, apart=None):
    contract = (((0,), (0,)), ((), ()))
    dist_sq = lax.dot_general(dist, target, contract, preferred_element_type=F32)
    flow = lax.dot_general(flux, target, contract, preferred_element_type=F32)
    if apart is not None:
        dist_sq = jnp.concatenate([dist_sq[:BAND_DEV] + apart, dist_sq[BAND_DEV:]], axis=0)
    tile = (flow * lax.rsqrt(dist_sq * dist_sq * dist_sq)).astype(BF16)
    return jnp.dot(density, tile, preferred_element_type=F32)


def chunk_features(corners, geometry, stage_ref):
    blocks = [
        source_features(
            corners[:, k * BLOCK : (k + 1) * BLOCK],
            geometry,
            (stage_ref.at[2 * k], stage_ref.at[2 * k + 1]),
        )
        for k in range(corners.shape[1] // BLOCK)
    ]
    return [jnp.concatenate([block[k] for block in blocks], axis=1) for k in range(2)]


def source_steps(
    corners_ref, first, density_refs, target_ref, total_ref, ready_refs, kept_refs, next_refs,
    geometry, stage_ref,
):
    src_dev = density_refs[0].shape[1]
    src_total = src_dev * len(density_refs)
    tgt_total = total_ref.shape[1]
    chunk = min(CHUNK, src_dev)
    steps = src_total // chunk
    tgt_step = max(
        step for step in range(BAND_DEV, TGT_STEP + 1, BAND_DEV) if tgt_total % step == 0
    )
    tgt_steps = tgt_total // tgt_step

    def make(turn):
        start = first * src_dev + turn * chunk
        return chunk_features(corners_ref[:, start : start + chunk], geometry, stage_ref)

    def apply(turn, dist, flux):
        here = pl.ds(turn * chunk, chunk)
        first = turn * chunk % src_dev
        density = density_refs[turn * chunk // src_dev][:, first : first + chunk]

        def some(step):
            cols = pl.ds(pl.multiple_of(step * tgt_step, 128), tgt_step)
            total_ref[:, cols] += pair_sums(dist, flux, target_ref[:, cols], density)

        if tgt_steps == 1:
            some(0)
        else:
            pl.loop(0, tgt_steps)(some)

    kept = [ref[...] for ref in ready_refs] if ready_refs else make(0)
    for turn in range(steps):
        for ref, values in zip(kept_refs, kept):
            ref[:, turn * chunk : (turn + 1) * chunk] = values
        apply(turn, *kept)
        following = make(turn + 1) if turn + 1 < steps or next_refs else None
        kept = following
    for ref, values in zip(next_refs, kept or ()):
        ref[...] = values


def partner(own, k, groups):
    return own ^ (groups - k) if groups & (groups - 1) == 0 else (own + groups - k) % groups


def start_corners(connectivity_ref, corners_ref, sems, firsts, count):
    copies = []
    for k, first in enumerate(firsts):
        copy = pltpu.make_async_copy(
            connectivity_ref.at[:, pl.ds(pl.multiple_of(first, 128), count)],
            corners_ref.at[:, pl.ds(k * count, count)],
            sems.at[k],
        )
        copy.start()
        copies.append(copy)
    return copies


def prepare_kernel(row_total, group, sizes, sample_ref, *refs):
    small_refs, connectivity_ref, refs = refs[:5], refs[5], refs[6:]
    (table_ref, origin_ref, far_ref, own_ref, src_corners), refs = refs[:5], refs[5:]
    small, (tgt_corners, tgt_stage_ref, stage_ref, small_sems, src_sems, tgt_sems) = refs[:5], refs[5:]
    lattice_ref, modes_ref, polar_ref, azim_ref, angles_ref = small
    pitch, first_cos, cycle_count = sizes
    src_dev = src_corners.shape[1] // group
    groups = row_total // group
    row = lax.axis_index("row")
    own_group = row // group
    place = row % group
    small_copies = []
    for k in range(5):
        small_copies.append(pltpu.make_async_copy(small_refs[k], small[k], small_sems.at[k]))
        small_copies[k].start()
    tgt_copies = start_corners(
        connectivity_ref, tgt_corners, tgt_sems,
        [(partner(own_group, k + 1, groups) * group + place) * src_dev for k in range(groups)], BAND_DEV,
    )
    src_copies = start_corners(
        connectivity_ref, src_corners, src_sems,
        [(own_group * group + (place ^ k)) * src_dev for k in range(group)], src_dev,
    )
    for copy in small_copies:
        copy.wait()
    radius = radius_table(
        sample_ref[0], lattice_ref[...], modes_ref[...], polar_ref[...], azim_ref[...], pitch
    )
    rows = angles_ref.shape[0]
    origin_ref[0:rows] = angles_ref[...]
    levels = heights(radius[0:1], radius[cycle_count - 1 : cycle_count], first_cos)
    for k, level in enumerate(levels):
        origin_ref[rows + k : rows + k + 1] = jnp.broadcast_to(level, (1, 128))
    table_ref[...] = radius
    for copy in tgt_copies + src_copies:
        copy.wait()
    geometry = (table_ref, angles_ref, cycle_count, levels)
    found = [
        target_features(tgt_corners[:, first : first + BLOCK], geometry, tgt_stage_ref)
        for first in range(0, tgt_corners.shape[1], BLOCK)
    ]
    found = jnp.concatenate(found, axis=1)
    far_ref[...] = found[:, :-BAND_DEV]
    own_ref[...] = found[:, -BAND_DEV:]


def sources_kernel(first, count, cycle_count, corners_ref, table_ref, origin_ref, far_ref, *refs):
    ready_refs, refs = (refs[:2], refs[2:]) if first else ((), refs)
    part_refs, refs = (refs[:1], refs[1:]) if first else ((), refs)
    density_refs, (*sums_refs, total_ref, stage_ref) = refs[:count], refs[count:]
    sums_refs, next_refs = (sums_refs, ()) if first else (sums_refs[:-2], sums_refs[-2:])
    sums_refs, kept_refs = sums_refs[:-2], sums_refs[-2:]
    rows = origin_ref.shape[0] - 8
    levels = [origin_ref[rows + k : rows + k + 1, 0:1] for k in range(6)]
    geometry = (table_ref, origin_ref, cycle_count, levels)
    if part_refs:
        total_ref[...] = part_refs[0][:, : total_ref.shape[1]]
    else:
        total_ref[...] = jnp.zeros_like(total_ref)
    source_steps(
        corners_ref, first, density_refs, far_ref, total_ref, ready_refs, kept_refs, next_refs,
        geometry, stage_ref,
    )
    width = sums_refs[0].shape[1]
    for k, ref in enumerate(sums_refs):
        ref[...] = total_ref[:, k * width : (k + 1) * width].astype(ref.dtype)


def kept_kernel(own, count, dist_ref, flux_ref, target_ref, *refs):
    density_refs, (*part_refs, sums_ref) = refs[:count], refs[count:]
    src_dev = density_refs[0].shape[1]
    target = target_ref[:, -BAND_DEV:]
    apart = None
    if own:
        diagonal = lax.broadcasted_iota(
            jnp.int32, (BAND_DEV, BAND_DEV), 0
        ) == lax.broadcasted_iota(jnp.int32, (BAND_DEV, BAND_DEV), 1)
        apart = jnp.where(diagonal, 1e30, 0.0)
    total = part_refs[0][:, -BAND_DEV:] if part_refs else None
    step = KEPT_STEP
    for first in range(0, count * src_dev, step):
        here = slice(first, first + step)
        inside = slice(first % src_dev, first % src_dev + step)
        sums = pair_sums(
            dist_ref[:, here], flux_ref[:, here], target, density_refs[first // src_dev][:, inside],
            None if first else apart,
        )
        total = sums if total is None else total + sums
    sums_ref[...] = total.astype(sums_ref.dtype)


def per_device(sample_index, lattice_vector, mode_table, connectivity, density):
    columns, src_dev = density.shape
    row_total = lax.axis_size("row")
    group = 4
    near = 2
    groups = row_total // group
    cycle_count = src_dev * row_total // (2 * NPH) + 1
    pitch, first_cos, tables = trig_tables(cycle_count)
    sizes = (pitch, first_cos, cycle_count)
    far_total = (groups - 1) * BAND_DEV
    vmem = pl.BlockSpec(memory_space=pltpu.VMEM)
    hbm = pl.BlockSpec(memory_space=pltpu.HBM)
    params = pltpu.CompilerParams(vmem_limit_bytes=VMEM)
    def moved(array, target_of):
        return lax.ppermute(array, "row", [(r, target_of(r)) for r in range(row_total)])

    densities = [density, moved(density, lambda r: r ^ 1), moved(density, lambda r: r ^ 2)]

    def shape(*dims, dtype=BF16):
        return jax.ShapeDtypeStruct(dims, dtype)

    def in_hbm(array):
        return pltpu.with_memory_space_constraint(array, pltpu.HBM)

    def cost(sources, targets):
        return pl.CostEstimate(
            flops=2 * sources * targets * 256 * 3, bytes_accessed=1 << 20, transcendentals=0
        )

    small = [lattice_vector.reshape(1, -1), mode_table, *map(jnp.asarray, tables)]
    stage = pltpu.VMEM((2 * min(CHUNK, src_dev) // BLOCK, 8 * FEATS, 128), F32)
    ready_shapes = [shape(FEATS, min(CHUNK, src_dev))] * 2
    table, origins, tgt_far, tgt_own, corners = pl.pallas_call(
        lambda *refs: prepare_kernel(row_total, group, sizes, *refs),
        out_shape=[
            shape(pitch, NPH, dtype=F32),
            shape(tables[2].shape[0] + 8, 128, dtype=F32),
            shape(FEATS, far_total),
            shape(FEATS, BAND_DEV),
            shape(3, group * src_dev, dtype=jnp.int32),
        ],
        in_specs=[pl.BlockSpec(memory_space=pltpu.SMEM)] + [hbm] * 6,
        out_specs=[vmem] * 5,
        scratch_shapes=[pltpu.VMEM(array.shape, array.dtype) for array in small]
        + [
            pltpu.VMEM((3, groups * BAND_DEV), jnp.int32),
            pltpu.VMEM((8 * FEATS, 128), F32),
            stage,
            pltpu.SemaphoreType.DMA((5,)),
            pltpu.SemaphoreType.DMA((group,)),
            pltpu.SemaphoreType.DMA((groups,)),
        ],
        compiler_params=params,
        cost_estimate=cost(1024, 256),
        name="prepare",
    )(sample_index, *[in_hbm(array) for array in (*small, connectivity)])

    def sources(first, blocks, ready, part, total, sums):
        handed_on = [] if first else ready_shapes
        *sums, dist, flux = pl.pallas_call(
            lambda *refs: sources_kernel(first, len(blocks), cycle_count, *refs),
            out_shape=sums + [shape(FEATS, len(blocks) * src_dev)] * 2 + handed_on,
            in_specs=[vmem] * (4 + len(ready) + len(part) + len(blocks)),
            out_specs=[vmem] * (len(sums) + 2 + len(handed_on)),
            scratch_shapes=[pltpu.VMEM((columns, total), F32), stage],
            compiler_params=params,
            cost_estimate=cost(len(blocks) * src_dev, total),
            name="other_sources" if first else "near_sources",
        )(corners, table, origins, tgt_far, *ready, *part, *blocks)
        return sums, (dist, flux)

    early = far_total - BAND_DEV
    (part, *near_features), ready = sources(
        0, densities[:near], [], [], far_total, [shape(columns, far_total, dtype=F32)]
    )
    relay, part = lax.optimization_barrier((densities[2], part))
    densities.append(moved(relay, lambda r: r ^ 1))
    sums, rest_features = sources(
        near, densities[near:], ready, [part], early, [shape(columns, BAND_DEV)] * (groups - 2)
    )

    def kept(features, target, blocks, own, part, dtype=F32):
        return pl.pallas_call(
            lambda *refs: kept_kernel(own, len(blocks), *refs),
            out_shape=shape(columns, BAND_DEV, dtype=dtype),
            in_specs=[vmem] * (3 + len(blocks) + len(part)),
            out_specs=vmem,
            compiler_params=params,
            cost_estimate=cost(len(blocks) * src_dev, BAND_DEV),
            name="own_first" if own else "late_targets" if dtype == BF16 else "own_last",
        )(*features, target, *blocks, *part)

    own_sums = kept(near_features, tgt_own, densities[:near], True, [])
    sums.append(kept(rest_features, tgt_far, densities[near:], False, [part], BF16))
    own_sums = kept(rest_features, tgt_own, densities[near:], False, [own_sums])
    total = 0.5 * density[:, :BAND_DEV].astype(F32) + own_sums
    for k, block in enumerate(sums):
        total = total + moved(
            block, lambda r, k=k: partner(r // group, k + 1, groups) * group + r % group
        ).astype(F32)
    return total.T


def solution(mesh):
    placed = (P("sample"), P(), P(), P(), P(None, "row"))
    return jax.shard_map(
        per_device,
        mesh=mesh,
        in_specs=placed,
        out_specs=P(("sample", "row"), None),
        check_vma=False,
    )
```

```python
import math

import jax
import jax.numpy as jnp
import numpy as np
from jax import lax
from jax.experimental import pallas as pl
from jax.experimental.pallas import tpu as pltpu
from jax.sharding import PartitionSpec as P

NLAT = 32768
NPH = 256
BAND_DEV = 256
FREQS = 32
FEATS = 64
BLOCK = 1024
CHUNK = 1024
TGT_STEP = 768
KEPT_STEP = 1024
VMEM = 30 << 20
F32 = jnp.float32
BF16 = jnp.bfloat16


def split(values):
    first = values.astype(BF16).astype(F32)
    rest = values - first
    second = rest.astype(BF16).astype(F32)
    third = (rest - second).astype(BF16).astype(F32)
    return [first, second, third]


def trig_tables(cycle_count):
    pitch = -(-cycle_count // 8) * 8
    cycle = np.arange(pitch)[:, None]
    polar = np.pi * (cycle + 1.0) / (cycle_count + 1) * (cycle < cycle_count)
    freq = np.arange(FREQS)[None, :]
    polar_table = np.concatenate([np.cos(freq * polar), -np.sin(freq * polar)], axis=0)
    azimuth = 2.0 * np.pi * np.arange(NPH)[None, :] / NPH
    azim_freq = np.arange(FREQS)[:, None] - FREQS // 2
    azim_table = np.concatenate([np.cos(azimuth * azim_freq), np.sin(azimuth * azim_freq)], axis=0)
    rows = -(-cycle_count // 128)
    ring = np.zeros((2, rows * 128))
    ring[0, :cycle_count] = np.sin(polar[:cycle_count, 0])
    ring[1, :cycle_count] = np.cos(polar[:cycle_count, 0])
    angles = np.concatenate(
        [ring.reshape(-1, 128), np.cos(azimuth).reshape(-1, 128), np.sin(azimuth).reshape(-1, 128)]
    )
    angles = np.concatenate([angles, np.zeros((-len(angles) % 8, 128))])
    first_cos = float(np.cos(np.pi / (cycle_count + 1)))
    tables = [polar_table, azim_table, angles]
    return pitch, first_cos, [table.astype(np.float32) for table in tables]


def radius_table(sample, lattice, modes, polar_table, azim_table, pitch):
    shifts = ((sample * lattice) & (NLAT - 1)).astype(F32) / NLAT - 0.5
    polar_freq = modes[0:1, :]
    azim_freq = modes[1:2, :]
    scale = (1 + polar_freq + jnp.abs(azim_freq)).astype(F32)
    coef = 0.8 * shifts / (scale * scale)
    numbers = lax.broadcasted_iota(jnp.int32, (FREQS, modes.shape[1]), 0)
    at_azim = numbers == azim_freq + FREQS // 2
    at_polar = jnp.where(numbers == polar_freq, 1.0, 0.0).astype(BF16)
    grid = None
    for part in split(coef):
        placed = lax.dot_general(
            at_polar,
            jnp.where(at_azim, part, 0.0).astype(BF16),
            (((1,), (1,)), ((), ())),
            preferred_element_type=F32,
        )
        grid = placed if grid is None else grid + placed
    exact = dict(precision=lax.Precision.HIGHEST, preferred_element_type=F32)
    both = jnp.dot(polar_table, grid, **exact)
    return jnp.exp(
        jnp.dot(both[:pitch], azim_table[:FREQS], **exact)
        + jnp.dot(both[pitch:], azim_table[FREQS:], **exact)
    )


def heights(first, last, first_cos):
    found, limits = [], []
    for ring, sign in ((first, first_cos), (last, -first_cos)):
        low = jnp.min(ring, axis=1, keepdims=True) * sign
        high = jnp.max(ring, axis=1, keepdims=True) * sign
        found += [0.25 * low + 0.75 * high, 0.75 * low + 0.25 * high]
        limits.append(0.5 * (low + high))
    return found + limits


def at_lanes(ref, row, first, lanes):
    values = jnp.broadcast_to(ref[row : row + 1, first : first + 128], lanes.shape)
    return jnp.take_along_axis(values, lanes, axis=1)


def radii(table_ref, column, cycles, cycle_count):
    lanes = column & 127
    right = column >= 128
    levels = (cycle_count - 1).bit_length()
    bits = [[(cycle & (1 << level)) != 0 for level in range(levels)] for cycle in cycles]

    def among(low, level):
        if level == 0:
            left = at_lanes(table_ref, low, 0, lanes)
            return [jnp.where(right, at_lanes(table_ref, low, 128, lanes), left)] * len(cycles)
        half = 1 << (level - 1)
        below = among(low, level - 1)
        if low + half >= cycle_count:
            return below
        above = among(low + half, level - 1)
        return [jnp.where(bit[level - 1], y, x) for bit, x, y in zip(bits, below, above)]

    return among(0, levels)


def angle_of(angles_ref, first, rows, index):
    lanes = index & 127
    found = at_lanes(angles_ref, first, 0, lanes)
    for row in range(1, rows):
        found = jnp.where(index >= 128 * row, at_lanes(angles_ref, first + row, 0, lanes), found)
    return found


def panels(corners, table_ref, angles_ref, cycle_count):
    zero, one, two = [
        jnp.concatenate([corners[c : c + 1, k * 128 : (k + 1) * 128] for k in range(8)], axis=0)
        for c in range(3)
    ]
    last = ((zero ^ one) & (NPH - 1)) == 0
    middle = ((zero ^ two) & (NPH - 1)) == 0
    turned = (
        jnp.where(last, two, jnp.where(middle, one, zero)),
        jnp.where(last, zero, jnp.where(middle, two, one)),
        jnp.where(last, one, jnp.where(middle, zero, two)),
    )
    cycles = [corner >> 8 for corner in turned]
    columns = [turned[0] & (NPH - 1), turned[1] & (NPH - 1)]
    radius = radii(table_ref, columns[0], cycles[:1], cycle_count) + radii(
        table_ref, columns[1], cycles[1:], cycle_count
    )
    rows = -(-cycle_count // 128)
    cos = [angle_of(angles_ref, 2 * rows, 2, column) for column in columns]
    sin = [angle_of(angles_ref, 2 * rows + 2, 2, column) for column in columns]
    points = []
    for c in range(3):
        flat = radius[c] * angle_of(angles_ref, 0, rows, cycles[c])
        side = min(c, 1)
        points.append(
            (flat * cos[side], flat * sin[side], radius[c] * angle_of(angles_ref, rows, rows, cycles[c]))
        )
    centers = [(points[0][d] + points[1][d] + points[2][d]) / 3.0 for d in range(3)]
    one = [points[1][d] - points[0][d] for d in range(3)]
    two = [points[2][d] - points[0][d] for d in range(3)]
    half = 0.5 / (4.0 * math.pi)
    areas = [
        half * (one[(d + 1) % 3] * two[(d + 2) % 3] - one[(d + 2) % 3] * two[(d + 1) % 3])
        for d in range(3)
    ]
    return centers, areas


def as_rows(values, stage_ref):
    for k, value in enumerate(values):
        stage_ref[k * 8 : (k + 1) * 8, :] = value
    blocks = [stage_ref[pl.ds(k, len(values), stride=8), :].astype(BF16) for k in range(8)]
    return jnp.concatenate(blocks, axis=1)


def left_pieces(value):
    one, two, three = split(value)
    return [one, one, one, two, two, three]


def right_pieces(value):
    one, two, three = split(value)
    return [one, two, three, one, two, one]


def padded(rows):
    return rows + [jnp.zeros((8, 128), F32)] * (FEATS - len(rows))


def target_features(corners, geometry, stage_ref):
    (x, y, z), _ = panels(corners, *geometry[:3])
    ones = [jnp.ones((8, 128), F32)] * 3
    rows = left_pieces(x) + left_pieces(y) + split(x * x + y * y) + ones
    for height in geometry[3][:4]:
        rise = z - height
        rows += left_pieces(rise) + split(rise * rise)
    return as_rows(padded(rows), stage_ref)


def source_features(corners, geometry, stage_refs):
    (x, y, z), areas = panels(corners, *geometry[:3])
    *levels, north, south = geometry[3]
    upper = z >= 0.0
    places = [z >= north, upper & (z < north), z <= south, ~upper & (z > south)]
    height = jnp.where(
        upper, jnp.where(places[0], levels[0], levels[1]), jnp.where(places[2], levels[2], levels[3])
    )
    rise = z - height
    zeros = jnp.zeros((8, 128), F32)
    square = x * x + y * y + rise * rise
    level = x * areas[0] + y * areas[1] + rise * areas[2]
    found = []
    for (a, b, c), flat, last, stage_ref in (
        ((-2.0 * x, -2.0 * y, -2.0 * rise), zeros + 1.0, square, stage_refs[0]),
        (areas, zeros, -level, stage_refs[1]),
    ):
        rows = right_pieces(a) + right_pieces(b) + [flat] * 3 + split(last)
        along = right_pieces(c) + [flat] * 3
        for place in places:
            rows += [jnp.where(place, row, 0.0) for row in along]
        found.append(as_rows(padded(rows), stage_ref))
    return found


def pair_sums(dist, flux, target, density, apart=None):
    contract = (((0,), (0,)), ((), ()))
    dist_sq = lax.dot_general(dist, target, contract, preferred_element_type=F32)
    flow = lax.dot_general(flux, target, contract, preferred_element_type=F32)
    if apart is not None:
        dist_sq = jnp.concatenate([dist_sq[:BAND_DEV] + apart, dist_sq[BAND_DEV:]], axis=0)
    tile = (flow * lax.rsqrt(dist_sq * dist_sq * dist_sq)).astype(BF16)
    return jnp.dot(density, tile, preferred_element_type=F32)


def chunk_features(corners, geometry, stage_ref):
    blocks = [
        source_features(
            corners[:, k * BLOCK : (k + 1) * BLOCK],
            geometry,
            (stage_ref.at[2 * k], stage_ref.at[2 * k + 1]),
        )
        for k in range(corners.shape[1] // BLOCK)
    ]
    return [jnp.concatenate([block[k] for block in blocks], axis=1) for k in range(2)]


def source_steps(
    corners_ref, first, density_refs, target_ref, total_ref, ready_refs, kept_refs, next_refs,
    geometry, stage_ref,
):
    src_dev = density_refs[0].shape[1]
    src_total = src_dev * len(density_refs)
    tgt_total = total_ref.shape[1]
    chunk = min(CHUNK, src_dev)
    steps = src_total // chunk
    tgt_step = max(
        step for step in range(BAND_DEV, TGT_STEP + 1, BAND_DEV) if tgt_total % step == 0
    )
    tgt_steps = tgt_total // tgt_step

    def make(turn):
        start = first * src_dev + turn * chunk
        return chunk_features(corners_ref[:, start : start + chunk], geometry, stage_ref)

    def apply(turn, dist, flux):
        here = pl.ds(turn * chunk, chunk)
        first = turn * chunk % src_dev
        density = density_refs[turn * chunk // src_dev][:, first : first + chunk]

        def some(step):
            cols = pl.ds(pl.multiple_of(step * tgt_step, 128), tgt_step)
            total_ref[:, cols] += pair_sums(dist, flux, target_ref[:, cols], density)

        if tgt_steps == 1:
            some(0)
        else:
            pl.loop(0, tgt_steps)(some)

    kept = [ref[...] for ref in ready_refs] if ready_refs else make(0)
    for turn in range(steps):
        for ref, values in zip(kept_refs, kept):
            ref[:, turn * chunk : (turn + 1) * chunk] = values
        following = make(turn + 1) if turn + 1 < steps or next_refs else None
        apply(turn, *kept)
        kept = following
    for ref, values in zip(next_refs, kept or ()):
        ref[...] = values


def partner(own, k, groups):
    return own ^ (groups - k) if groups & (groups - 1) == 0 else (own + groups - k) % groups


def start_corners(connectivity_ref, corners_ref, sems, firsts, count):
    copies = []
    for k, first in enumerate(firsts):
        copy = pltpu.make_async_copy(
            connectivity_ref.at[:, pl.ds(pl.multiple_of(first, 128), count)],
            corners_ref.at[:, pl.ds(k * count, count)],
            sems.at[k],
        )
        copy.start()
        copies.append(copy)
    return copies


def prepare_kernel(row_total, group, sizes, sample_ref, *refs):
    small_refs, connectivity_ref, refs = refs[:5], refs[5], refs[6:]
    (table_ref, origin_ref, far_ref, own_ref, src_corners), refs = refs[:5], refs[5:]
    small, (tgt_corners, tgt_stage_ref, stage_ref, small_sems, src_sems, tgt_sems) = refs[:5], refs[5:]
    lattice_ref, modes_ref, polar_ref, azim_ref, angles_ref = small
    pitch, first_cos, cycle_count = sizes
    src_dev = src_corners.shape[1] // group
    groups = row_total // group
    row = lax.axis_index("row")
    own_group = row // group
    place = row % group
    small_copies = []
    for k in range(5):
        small_copies.append(pltpu.make_async_copy(small_refs[k], small[k], small_sems.at[k]))
        small_copies[k].start()
    tgt_copies = start_corners(
        connectivity_ref, tgt_corners, tgt_sems,
        [(partner(own_group, k + 1, groups) * group + place) * src_dev for k in range(groups)], BAND_DEV,
    )
    src_copies = start_corners(
        connectivity_ref, src_corners, src_sems,
        [(own_group * group + (place ^ k)) * src_dev for k in range(group)], src_dev,
    )
    for copy in small_copies:
        copy.wait()
    radius = radius_table(
        sample_ref[0], lattice_ref[...], modes_ref[...], polar_ref[...], azim_ref[...], pitch
    )
    rows = angles_ref.shape[0]
    origin_ref[0:rows] = angles_ref[...]
    levels = heights(radius[0:1], radius[cycle_count - 1 : cycle_count], first_cos)
    for k, level in enumerate(levels):
        origin_ref[rows + k : rows + k + 1] = jnp.broadcast_to(level, (1, 128))
    table_ref[...] = radius
    for copy in tgt_copies + src_copies:
        copy.wait()
    geometry = (table_ref, angles_ref, cycle_count, levels)
    found = [
        target_features(tgt_corners[:, first : first + BLOCK], geometry, tgt_stage_ref)
        for first in range(0, tgt_corners.shape[1], BLOCK)
    ]
    found = jnp.concatenate(found, axis=1)
    far_ref[...] = found[:, :-BAND_DEV]
    own_ref[...] = found[:, -BAND_DEV:]


def sources_kernel(first, count, cycle_count, corners_ref, table_ref, origin_ref, far_ref, *refs):
    ready_refs, refs = (refs[:2], refs[2:]) if first else ((), refs)
    part_refs, refs = (refs[:1], refs[1:]) if first else ((), refs)
    density_refs, (*sums_refs, total_ref, stage_ref) = refs[:count], refs[count:]
    sums_refs, next_refs = (sums_refs, ()) if first else (sums_refs[:-2], sums_refs[-2:])
    sums_refs, kept_refs = sums_refs[:-2], sums_refs[-2:]
    rows = origin_ref.shape[0] - 8
    levels = [origin_ref[rows + k : rows + k + 1, 0:1] for k in range(6)]
    geometry = (table_ref, origin_ref, cycle_count, levels)
    if part_refs:
        total_ref[...] = part_refs[0][:, : total_ref.shape[1]]
    else:
        total_ref[...] = jnp.zeros_like(total_ref)
    source_steps(
        corners_ref, first, density_refs, far_ref, total_ref, ready_refs, kept_refs, next_refs,
        geometry, stage_ref,
    )
    width = sums_refs[0].shape[1]
    for k, ref in enumerate(sums_refs):
        ref[...] = total_ref[:, k * width : (k + 1) * width].astype(ref.dtype)


def kept_kernel(own, count, dist_ref, flux_ref, target_ref, *refs):
    density_refs, (*part_refs, sums_ref) = refs[:count], refs[count:]
    src_dev = density_refs[0].shape[1]
    target = target_ref[:, -BAND_DEV:]
    apart = None
    if own:
        diagonal = lax.broadcasted_iota(
            jnp.int32, (BAND_DEV, BAND_DEV), 0
        ) == lax.broadcasted_iota(jnp.int32, (BAND_DEV, BAND_DEV), 1)
        apart = jnp.where(diagonal, 1e30, 0.0)
    total = part_refs[0][:, -BAND_DEV:] if part_refs else None
    if own:
        total = 0.5 * density_refs[0][:, :BAND_DEV].astype(F32)
    step = KEPT_STEP
    for first in range(0, count * src_dev, step):
        here = slice(first, first + step)
        inside = slice(first % src_dev, first % src_dev + step)
        sums = pair_sums(
            dist_ref[:, here], flux_ref[:, here], target, density_refs[first // src_dev][:, inside],
            None if first else apart,
        )
        total = sums if total is None else total + sums
    sums_ref[...] = total.astype(sums_ref.dtype)


def per_device(sample_index, lattice_vector, mode_table, connectivity, density):
    columns, src_dev = density.shape
    row_total = lax.axis_size("row")
    group = 4
    near = 2
    groups = row_total // group
    cycle_count = src_dev * row_total // (2 * NPH) + 1
    pitch, first_cos, tables = trig_tables(cycle_count)
    sizes = (pitch, first_cos, cycle_count)
    far_total = (groups - 1) * BAND_DEV
    vmem = pl.BlockSpec(memory_space=pltpu.VMEM)
    hbm = pl.BlockSpec(memory_space=pltpu.HBM)
    params = pltpu.CompilerParams(vmem_limit_bytes=VMEM)
    def moved(array, target_of):
        return lax.ppermute(array, "row", [(r, target_of(r)) for r in range(row_total)])

    densities = [density, moved(density, lambda r: r ^ 1), moved(density, lambda r: r ^ 2)]

    def shape(*dims, dtype=BF16):
        return jax.ShapeDtypeStruct(dims, dtype)

    def in_hbm(array):
        return pltpu.with_memory_space_constraint(array, pltpu.HBM)

    def cost(sources, targets):
        return pl.CostEstimate(
            flops=2 * sources * targets * 256 * 3, bytes_accessed=1 << 20, transcendentals=0
        )

    small = [lattice_vector.reshape(1, -1), mode_table, *map(jnp.asarray, tables)]
    stage = pltpu.VMEM((2 * min(CHUNK, src_dev) // BLOCK, 8 * FEATS, 128), F32)
    ready_shapes = [shape(FEATS, min(CHUNK, src_dev))] * 2
    table, origins, tgt_far, tgt_own, corners = pl.pallas_call(
        lambda *refs: prepare_kernel(row_total, group, sizes, *refs),
        out_shape=[
            shape(pitch, NPH, dtype=F32),
            shape(tables[2].shape[0] + 8, 128, dtype=F32),
            shape(FEATS, far_total),
            shape(FEATS, BAND_DEV),
            shape(3, group * src_dev, dtype=jnp.int32),
        ],
        in_specs=[pl.BlockSpec(memory_space=pltpu.SMEM)] + [hbm] * 6,
        out_specs=[vmem] * 5,
        scratch_shapes=[pltpu.VMEM(array.shape, array.dtype) for array in small]
        + [
            pltpu.VMEM((3, groups * BAND_DEV), jnp.int32),
            pltpu.VMEM((8 * FEATS, 128), F32),
            stage,
            pltpu.SemaphoreType.DMA((5,)),
            pltpu.SemaphoreType.DMA((group,)),
            pltpu.SemaphoreType.DMA((groups,)),
        ],
        compiler_params=params,
        cost_estimate=cost(1024, 256),
        name="prepare",
    )(sample_index, *[in_hbm(array) for array in (*small, connectivity)])

    def sources(first, blocks, ready, part, total, sums):
        handed_on = [] if first else ready_shapes
        *sums, dist, flux = pl.pallas_call(
            lambda *refs: sources_kernel(first, len(blocks), cycle_count, *refs),
            out_shape=sums + [shape(FEATS, len(blocks) * src_dev)] * 2 + handed_on,
            in_specs=[vmem] * (4 + len(ready) + len(part) + len(blocks)),
            out_specs=[vmem] * (len(sums) + 2 + len(handed_on)),
            scratch_shapes=[pltpu.VMEM((columns, total), F32), stage],
            compiler_params=params,
            cost_estimate=cost(len(blocks) * src_dev, total),
            name="other_sources" if first else "near_sources",
        )(corners, table, origins, tgt_far, *ready, *part, *blocks)
        return sums, (dist, flux)

    early = far_total - BAND_DEV
    (part, *near_features), ready = sources(
        0, densities[:near], [], [], far_total, [shape(columns, far_total, dtype=F32)]
    )
    relay, part = lax.optimization_barrier((densities[2], part))
    densities.append(moved(relay, lambda r: r ^ 1))
    sums, rest_features = sources(
        near, densities[near:], ready, [part], early, [shape(columns, BAND_DEV)] * (groups - 2)
    )

    def kept(features, target, blocks, own, part, dtype=F32):
        return pl.pallas_call(
            lambda *refs: kept_kernel(own, len(blocks), *refs),
            out_shape=shape(columns, BAND_DEV, dtype=dtype),
            in_specs=[vmem] * (3 + len(blocks) + len(part)),
            out_specs=vmem,
            compiler_params=params,
            cost_estimate=cost(len(blocks) * src_dev, BAND_DEV),
            name="own_first" if own else "late_targets" if dtype == BF16 else "own_last",
        )(*features, target, *blocks, *part)

    own_sums = kept(near_features, tgt_own, densities[:near], True, [])
    sums.append(kept(rest_features, tgt_far, densities[near:], False, [part], BF16))
    own_sums = kept(rest_features, tgt_own, densities[near:], False, [own_sums])
    total = own_sums
    for k, block in enumerate(sums):
        total = total + moved(
            block, lambda r, k=k: partner(r // group, k + 1, groups) * group + r % group
        ).astype(F32)
    return total.T


def solution(mesh):
    placed = (P("sample"), P(), P(), P(), P(None, "row"))
    return jax.shard_map(
        per_device,
        mesh=mesh,
        in_specs=placed,
        out_specs=P(("sample", "row"), None),
        check_vma=False,
    )
```
